256 devices in a mesh: grp: 8 (over z), sp: 32 (over x, y, core).
Axes of the slice: x: 4, y: 4, z: 8, core: 2. Of those that a mesh axis runs over, the one named last changes fastest.
Arguments:
- queries: bfloat16 [32768, 4096], P(('grp', 'sp')), may hold values from -24 to 24
- keys: bfloat16 [32768, 512], P(('grp', 'sp')), may hold values from -24 to 24
- values: bfloat16 [32768, 512], P(('grp', 'sp')), may hold values from -6 to 6
- out_grad: bfloat16 [32768, 4096], P(('grp', 'sp')), may hold values from -6 to 6
- dest_group: int32 [32768], P(('grp', 'sp')), may hold values from 0 to 7, as said below
- dest_slot: int32 [32768], P(('grp', 'sp')), may hold values from 0 to 127, as said below
- group_lengths: int32 [8, 8], replicated, may hold values from 1 to 1024, as said below
Outputs:
- attn_out: bfloat16 [32768, 4096], P(('grp', 'sp'))
- q_grad: bfloat16 [32768, 4096], P(('grp', 'sp'))
- k_grad: bfloat16 [32768, 512], P(('grp', 'sp'))
- v_grad: bfloat16 [32768, 512], P(('grp', 'sp'))
The draws below stay inside these ranges and needn't reach their ends.
Inputs may be any that keep to these rules, and one draw needn't show every extreme that they name: `dest_group`: for each sp index s, the rows of the devices with that sp index together fill every slot 0 to 127 of every group's device with sp index s exactly once; from one device to one group go 0, 16 or 32 rows, and 32 is reached from every device. `dest_slot`: slots are distinct among the rows that one device receives. `group_lengths`: each row sums to 4096; no sequence is longer than 1024 rows, and every group holds one sequence of exactly 1024 rows.
All inputs are finite; a program needn't handle non-finite values.
Results may differ from the reference program's by a relative error of at most 0.012.
The reference program's roundings to bfloat16 on the way count: a program that leaves them out, or rounds other values in their place, can miss the bound.
Values may be sent and summed in bfloat16 or wider, within the bound.
No kernel may reach another device: no remote copies, remote signals or barrier semaphores. Data moves between devices by JAX's collectives and lax.ppermute only.
A program may use at most 128 MiB of HBM per device.

```python
import functools
import math
import jax
import jax.numpy as jnp
from jax import lax

QUERY_HEADS = 32
KEY_VALUE_HEADS = 4
HEAD_SIZE = 128
TOK_DEV = 128
SEQ_SLOTS = 8
SEQUENCE_GROUPS = 8
ROWS_PER_GROUP = 4096
TOKEN_TOTAL = 32768
N_SP = 32


def permutations(key, count, size):
    keys = jax.random.split(key, count)
    return jax.vmap(functools.partial(jax.random.permutation, x=size))(keys)


def routing_tables(key):
    spread = ROWS_PER_GROUP // TOK_DEV
    base = TOK_DEV // SEQUENCE_GROUPS
    keys = jax.random.split(key, 4)
    order = permutations(keys[0], spread, SEQUENCE_GROUPS).astype(jnp.int32)
    shift = jax.random.randint(keys[1], (spread, 1), 1, SEQUENCE_GROUPS)
    index = jnp.arange(SEQUENCE_GROUPS, dtype=jnp.int32)
    other = jnp.take_along_axis(order, (index[None, :] + shift) % SEQUENCE_GROUPS, axis=1)
    first = (order[:, :, None] == index[None, None, :]).astype(jnp.int32)
    second = (other[:, :, None] == index[None, None, :]).astype(jnp.int32)
    counts = base + base * first - base * second
    offsets = jnp.cumsum(counts, axis=1) - counts
    ends = jnp.cumsum(counts, axis=2)
    rows = jnp.arange(TOK_DEV, dtype=jnp.int32)
    target = jnp.sum((rows[None, None, :, None] >= ends[:, :, None, :]).astype(jnp.int32), axis=3)
    begin = jnp.take_along_axis(ends - counts, target, axis=2)
    slot_pre = jnp.take_along_axis(offsets, target, axis=2) + rows[None, None, :] - begin
    shuffle = permutations(keys[2], spread * SEQUENCE_GROUPS, TOK_DEV).astype(jnp.int32).reshape(spread, SEQUENCE_GROUPS, TOK_DEV)
    column = jnp.arange(spread, dtype=jnp.int32)[:, None, None]
    slot = shuffle[column, target, slot_pre]
    local = permutations(keys[3], spread * SEQUENCE_GROUPS, TOK_DEV).astype(jnp.int32).reshape(spread, SEQUENCE_GROUPS, TOK_DEV)
    source = jnp.arange(SEQUENCE_GROUPS, dtype=jnp.int32)[None, :, None]
    group_out = jnp.zeros((spread, SEQUENCE_GROUPS, TOK_DEV), jnp.int32).at[column, source, local].set(target)
    slot_out = jnp.zeros((spread, SEQUENCE_GROUPS, TOK_DEV), jnp.int32).at[column, source, local].set(slot)
    return (jnp.transpose(group_out, (1, 0, 2)).reshape(TOKEN_TOTAL), jnp.transpose(slot_out, (1, 0, 2)).reshape(TOKEN_TOTAL))


def draw_dest_group(key, part):
    tables = routing_tables(key)
    return tables[0].astype(jnp.int32)


def draw_dest_slot(key, part):
    tables = routing_tables(key)
    return tables[1].astype(jnp.int32)


def draw_group_lengths(key, part):
    key = jax.random.fold_in(key, 3)
    keys = jax.random.split(key, 2)
    longest = ROWS_PER_GROUP // 4
    remain = ROWS_PER_GROUP - longest
    weights = jax.random.randint(keys[0], (SEQUENCE_GROUPS, SEQ_SLOTS - 1), 1, 3).astype(jnp.int32)
    weight_sum = jnp.sum(weights, axis=1, keepdims=True)
    share = remain * weights // weight_sum
    left = remain - jnp.sum(share, axis=1, keepdims=True)
    index = jnp.arange(SEQ_SLOTS - 1, dtype=jnp.int32)[None, :]
    share = share + (index < left).astype(jnp.int32)
    lengths = jnp.concatenate([jnp.full((SEQUENCE_GROUPS, 1), longest, jnp.int32), share], axis=1)
    offset = jax.random.randint(keys[1], (SEQUENCE_GROUPS, 1), 0, SEQ_SLOTS)
    order = (jnp.arange(SEQ_SLOTS, dtype=jnp.int32)[None, :] + offset) % SEQ_SLOTS
    return jnp.take_along_axis(lengths, order, axis=1).astype(jnp.int32)


def draw_queries(key, part):
    key = jax.random.fold_in(key, 11)
    field_name = jnp.clip(jax.random.normal(key, (TOKEN_TOTAL, QUERY_HEADS, HEAD_SIZE)), -6.0, 6.0)
    return field_name.reshape(TOKEN_TOTAL, QUERY_HEADS * HEAD_SIZE).astype(jnp.bfloat16)


def draw_keys(key, part):
    key = jax.random.fold_in(key, 12)
    field_name = jnp.clip(jax.random.normal(key, (TOKEN_TOTAL, KEY_VALUE_HEADS, HEAD_SIZE)), -6.0, 6.0)
    return field_name.reshape(TOKEN_TOTAL, KEY_VALUE_HEADS * HEAD_SIZE).astype(jnp.bfloat16)


def shard_levels(stream_key, extent, cuts, low, top_value):
    loudness = 1.0
    for axis_at, parts in cuts:
        steps = jax.random.uniform(jax.random.fold_in(jax.random.fold_in(stream_key, 6), axis_at), (parts,), jnp.float32, low / len(cuts), top_value / len(cuts))
        loudness = loudness * jnp.repeat(jnp.exp(steps), extent[axis_at] // parts).reshape((-1,) + (1,) * (len(extent) - 1 - axis_at))
    return loudness


def centred(rng, extent, scale, bound, cuts=(), kind=jnp.bfloat16):
    factor_of = shard_levels(rng, extent, cuts, -0.22, 0.18) if cuts else 1.0
    values = jax.random.normal(rng, extent, jnp.float32) * scale * factor_of
    return jnp.minimum(jnp.maximum(values, -bound), bound).astype(kind)


def setup_inputs(seed: int = 0) -> dict:
    arg_keys = jax.random.split(jax.random.key(seed), 8)
    return {
        "queries": draw_queries(jax.random.fold_in(arg_keys[7], 71), 0),
        "keys": draw_keys(jax.random.fold_in(arg_keys[7], 71), 0),
        "values": centred(arg_keys[2], (TOKEN_TOTAL, KEY_VALUE_HEADS * HEAD_SIZE), 1.0, 6.0, ((0, 256),)),
        "out_grad": centred(arg_keys[3], (TOKEN_TOTAL, QUERY_HEADS * HEAD_SIZE), 1.0, 6.0, ((0, 256),)),
        "dest_group": draw_dest_group(jax.random.fold_in(arg_keys[7], 71), 0),
        "dest_slot": draw_dest_slot(jax.random.fold_in(arg_keys[7], 71), 0),
        "group_lengths": draw_group_lengths(jax.random.fold_in(arg_keys[7], 71), 0),
    }


def seq_layout(lengths, total):
    rows = jnp.arange(total, dtype=jnp.int32)
    lengths = lengths.astype(jnp.int32)
    ends = jnp.cumsum(lengths).astype(jnp.int32)
    starts = ends - lengths
    segment = lax.optimization_barrier(jnp.sum((rows[:, None] >= ends[None, :-1]).astype(jnp.int32), axis=1))
    slots = jnp.arange(lengths.shape[0], dtype=jnp.int32)
    begin = lax.optimization_barrier(jnp.sum(jnp.where(segment[:, None] == slots[None, :], starts[None, :], 0), axis=1))
    return (segment, rows - begin)

def rope_tables(position, head_dim):
    half = head_dim // 2
    freq = jnp.power(500000.0, -(2.0 / head_dim) * jnp.arange(half, dtype=jnp.float32))
    angle = position.astype(jnp.float32)[:, None] * freq[None, :]
    return (jnp.cos(angle), jnp.sin(angle))

def rotate(field_name, cosine, sine, sign):
    half = field_name.shape[1] // 2
    first = field_name[:, :half]
    second = field_name[:, half:]
    return jnp.concatenate([first * cosine - sign * second * sine, second * cosine + sign * first * sine], axis=1)

def head_pass(query, key_rows, value_rows, grad_rows, segment, cosine, sine):
    total, head_dim = query.shape
    scale = 1.0 / math.sqrt(head_dim)
    q_rot = rotate(query.astype(jnp.float32), cosine, sine, 1.0).astype(jnp.bfloat16)
    k_rot = rotate(key_rows.astype(jnp.float32), cosine, sine, 1.0).astype(jnp.bfloat16)
    block = min(512, total)
    reach = total // 4
    rows = jnp.arange(total, dtype=jnp.int32)
    key_grad = jnp.zeros((total, head_dim), jnp.float32)
    value_grad = jnp.zeros((total, head_dim), jnp.float32)
    outputs = []
    q_parts = []
    for index in range(total // block):
        low = index * block
        high = low + block
        start = max(0, low - reach)
        q_block = q_rot[low:high]
        k_block = k_rot[start:high]
        v_block = value_rows[start:high]
        g_block = grad_rows[low:high]
        score = jnp.dot(q_block, k_block.T, preferred_element_type=jnp.float32) * scale
        allowed = (rows[None, start:high] <= rows[low:high, None]) & (segment[None, start:high] == segment[low:high, None])
        score = jnp.where(allowed, score, -jnp.inf)
        top = lax.optimization_barrier(jnp.max(score, axis=1, keepdims=True))
        weight = jnp.exp(score - top)
        weight = weight / lax.optimization_barrier(jnp.sum(weight, axis=1, keepdims=True))
        weight_low = weight.astype(jnp.bfloat16)
        mixed = jnp.dot(weight_low, v_block, preferred_element_type=jnp.float32)
        outputs.append(mixed.astype(jnp.bfloat16))
        delta = lax.optimization_barrier(jnp.sum(g_block.astype(jnp.float32) * mixed, axis=1, keepdims=True))
        weight_grad = jnp.dot(g_block, v_block.T, preferred_element_type=jnp.float32)
        score_grad = (weight * (weight_grad - delta)).astype(jnp.bfloat16)
        q_parts.append(jnp.dot(score_grad, k_block, preferred_element_type=jnp.float32) * scale)
        key_grad = key_grad.at[start:high].add(jnp.dot(score_grad.T, q_block, preferred_element_type=jnp.float32) * scale)
        value_grad = value_grad.at[start:high].add(jnp.dot(weight_low.T, g_block, preferred_element_type=jnp.float32))
    q_grad = rotate(jnp.concatenate(q_parts, axis=0), cosine, sine, -1.0).astype(jnp.bfloat16)
    k_term = rotate(key_grad, cosine, sine, -1.0).astype(jnp.bfloat16)
    return (jnp.concatenate(outputs, axis=0), q_grad, k_term, value_grad.astype(jnp.bfloat16))

def reference(queries, keys, values, out_grad, dest_group, dest_slot, group_lengths):
    rows = jnp.arange(TOKEN_TOTAL, dtype=jnp.int32)
    where_to = dest_group * ROWS_PER_GROUP + rows // TOK_DEV % N_SP * TOK_DEV + dest_slot
    head_ratio = QUERY_HEADS // KEY_VALUE_HEADS

    def into_sequence_groups(field_name, heads):
        placed = jnp.zeros_like(field_name).at[where_to].set(field_name)
        return placed.reshape(SEQUENCE_GROUPS, ROWS_PER_GROUP, heads, HEAD_SIZE)
    q_groups = into_sequence_groups(queries, QUERY_HEADS)
    key_by_group = into_sequence_groups(keys, KEY_VALUE_HEADS)
    value_by_group = into_sequence_groups(values, KEY_VALUE_HEADS)
    g_groups = into_sequence_groups(out_grad, QUERY_HEADS)

    def pick(field_name, index):
        return lax.dynamic_index_in_dim(field_name, index, 1, keepdims=False)

    def per_group(items):
        q_all, k_all, v_all, g_all, lengths = items
        segment, position = seq_layout(lengths, ROWS_PER_GROUP)
        cosine, sine = rope_tables(position, HEAD_SIZE)

        def per_head(head):
            shared = head // head_ratio
            return head_pass(pick(q_all, head), pick(k_all, shared), pick(v_all, shared), pick(g_all, head), segment, cosine, sine)
        return lax.map(per_head, jnp.arange(QUERY_HEADS, dtype=jnp.int32))
    result = lax.map(per_group, (q_groups, key_by_group, value_by_group, g_groups, group_lengths))

    def to_rows(field_name):
        flat = jnp.transpose(field_name, (0, 2, 1, 3)).reshape(TOKEN_TOTAL, -1)
        return flat[where_to]

    def merge_heads(field_name):
        summed_result = lax.optimization_barrier(jnp.sum(field_name.astype(jnp.float32).reshape(SEQUENCE_GROUPS, KEY_VALUE_HEADS, head_ratio, ROWS_PER_GROUP, HEAD_SIZE), axis=2))
        return to_rows(summed_result.astype(jnp.bfloat16))
    return (to_rows(result[0]), to_rows(result[1]), merge_heads(result[2]), merge_heads(result[3]))
```

```python
import functools
import math

import jax
import jax.numpy as jnp
from jax import lax
from jax.experimental import pallas as pl
from jax.experimental.pallas import tpu as pltpu
from jax.sharding import PartitionSpec as P

HEAD = 128
TOK = 128
PARTS = 8
QUARTER = PARTS * TOK
BLOCK_Q = 256
BLOCK_K = 256
SPAN = QUARTER // BLOCK_K + 1
LOG2E = 1.0 / math.log(2.0)
CHUNKS = 1
VMEM = 48 * 1024 * 1024


def dot(left, right, left_dim, right_dim):
    return lax.dot_general(
        left, right, (((left_dim,), (right_dim,)), ((), ())), preferred_element_type=jnp.float32
    )


def call(body, out_shape, args, specs, flops, scratch=()):
    return pl.pallas_call(
        body,
        out_shape=out_shape,
        in_specs=specs,
        out_specs=jax.tree.map(lambda _: pl.BlockSpec(memory_space=pltpu.VMEM), out_shape),
        scratch_shapes=scratch,
        compiler_params=pltpu.CompilerParams(vmem_limit_bytes=VMEM),
        cost_estimate=pl.CostEstimate(flops=flops, bytes_accessed=4 << 20, transcendentals=0),
    )(*args)


IN_VMEM = pl.BlockSpec(memory_space=pltpu.VMEM)
IN_SMEM = pl.BlockSpec(memory_space=pltpu.SMEM)


def place_body(code_ref, x_ref, out_ref):
    width = x_ref.shape[2]
    rows = x_ref[:, :TOK, :].reshape(QUARTER, width)
    slots = lax.broadcasted_iota(jnp.int32, (TOK, TOK), 0)
    for group in range(PARTS):
        hot = jnp.concatenate(
            [
                jnp.where(slots + group * TOK == code_ref[source : source + 1, :], 1.0, 0.0)
                for source in range(PARTS)
            ],
            axis=1,
        ).astype(jnp.bfloat16)
        out_ref[group] = dot(hot, rows, 1, 0).astype(out_ref.dtype)


def place(code, field):
    width = field.shape[2]
    return call(
        place_body,
        jax.ShapeDtypeStruct((PARTS, TOK, width), field.dtype),
        (code, field),
        [IN_VMEM, IN_VMEM],
        2 * QUARTER * QUARTER * width,
    )


def unplace_body(code_ref, x_ref, out_ref):
    width = x_ref.shape[2]
    rows = x_ref[...].reshape(QUARTER, width)
    spots = lax.broadcasted_iota(jnp.int32, (TOK, QUARTER), 1)
    for source in range(PARTS):
        hot = jnp.where(spots == code_ref[:, source : source + 1], 1.0, 0.0).astype(jnp.bfloat16)
        out_ref[source] = dot(hot, rows, 1, 0).astype(out_ref.dtype)


def unplace(code_columns, field):
    width = field.shape[2]
    return call(
        unplace_body,
        jax.ShapeDtypeStruct((PARTS, TOK, width), field.dtype),
        (code_columns, field),
        [IN_VMEM, IN_VMEM],
        2 * QUARTER * QUARTER * width,
    )


def turn(field, cosine, sine):
    return field * cosine + pltpu.roll(field, HEAD // 2, 1) * sine


def attend_body(
    heads, begin_ref, first_ref, qg_ref, own_ref, before_ref, cos_ref, sin_ref,
    og_ref, dkv_ref, k_rot, v_all, q_rot, g_all, low_p, s_ref, w_ref,
):
    scale = 1.0 / math.sqrt(HEAD)
    rows = heads * BLOCK_Q
    for half, source in ((0, before_ref), (1, own_ref)):
        at = pl.ds(half * QUARTER, QUARTER)
        k_rot[at, :] = turn(
            source[:, :HEAD].astype(jnp.float32), cos_ref[at, :], sin_ref[at, :]
        ).astype(jnp.bfloat16)
        v_all[at, :] = source[:, HEAD:]
    dkv_ref[...] = jnp.zeros_like(dkv_ref)
    for block in range(QUARTER // BLOCK_Q):
        low = block * BLOCK_Q
        cosine = cos_ref[pl.ds(QUARTER + low, BLOCK_Q), :]
        sine = sin_ref[pl.ds(QUARTER + low, BLOCK_Q), :]
        for head in range(heads):
            at = pl.ds(head * BLOCK_Q, BLOCK_Q)
            columns = pl.ds(head * HEAD, HEAD)
            query = qg_ref[pl.ds(low, BLOCK_Q), columns].astype(jnp.float32)
            q_rot[at, :] = turn(query, cosine, sine).astype(jnp.bfloat16)
            g_all[at, :] = qg_ref[pl.ds(low, BLOCK_Q), pl.ds((heads + head) * HEAD, HEAD)]
        start = begin_ref[pl.ds(low, BLOCK_Q), :]
        end = lax.broadcasted_iota(jnp.int32, (BLOCK_Q, 1), 0) + (QUARTER + low)
        first = first_ref[block]
        count = QUARTER // BLOCK_K + (block + 1) * BLOCK_Q // BLOCK_K - first

        def key_rows(step):
            return pl.ds(pl.multiple_of((first + step) * BLOCK_K, BLOCK_K), BLOCK_K)

        def score_step(step, top):
            score = dot(q_rot[...], k_rot[key_rows(step), :], 1, 1)
            key = lax.broadcasted_iota(jnp.int32, (BLOCK_Q, BLOCK_K), 1) + (first + step) * BLOCK_K
            allowed = (key >= start) & (key <= end)
            score = jnp.where(
                allowed[None], score.reshape(heads, BLOCK_Q, BLOCK_K), -jnp.inf
            ).reshape(rows, BLOCK_K)
            s_ref[step] = score
            return jnp.maximum(top, jnp.max(score, axis=1, keepdims=True))

        top = lax.fori_loop(0, count, score_step, jnp.full((rows, 1), -jnp.inf, jnp.float32))

        def exp_step(step, total):
            weight = jnp.exp2((s_ref[step] - top) * (scale * LOG2E))
            s_ref[step] = weight
            return total + jnp.sum(weight, axis=1, keepdims=True)

        total = lax.fori_loop(0, count, exp_step, jnp.zeros((rows, 1), jnp.float32))
        inverse = 1.0 / total

        def mix_step(step, mixed):
            weight = s_ref[step] * inverse
            s_ref[step] = weight
            weight_low = weight.astype(jnp.bfloat16)
            low_p[step] = weight_low
            return mixed + dot(weight_low, v_all[key_rows(step), :], 1, 0)

        mixed = lax.fori_loop(0, count, mix_step, jnp.zeros((rows, HEAD), jnp.float32))
        delta = jnp.sum(g_all[...].astype(jnp.float32) * mixed, axis=1, keepdims=True)

        def grad_step(step, q_grad):
            at = key_rows(step)
            weight_grad = dot(g_all[...], v_all[at, :], 1, 1)
            score_grad = (s_ref[step] * (weight_grad - delta)).astype(jnp.bfloat16)
            w_ref[...] = score_grad
            dkv_ref[at, :HEAD] += dot(w_ref[...], q_rot[...], 0, 0)
            dkv_ref[at, HEAD:] += dot(low_p[step], g_all[...], 0, 0)
            return q_grad + dot(score_grad, k_rot[at, :], 1, 0)

        q_grad = lax.fori_loop(0, count, grad_step, jnp.zeros((rows, HEAD), jnp.float32))
        for head in range(heads):
            at = slice(head * BLOCK_Q, (head + 1) * BLOCK_Q)
            og_ref[pl.ds(low, BLOCK_Q), pl.ds(head * HEAD, HEAD)] = mixed[at].astype(jnp.bfloat16)
            og_ref[pl.ds(low, BLOCK_Q), pl.ds((heads + head) * HEAD, HEAD)] = turn(
                q_grad[at] * scale, cosine, -sine
            ).astype(jnp.bfloat16)
    dkv_ref[:, :HEAD] = turn(dkv_ref[:, :HEAD] * scale, cos_ref[...], -sin_ref[...])


def attend(heads, begin, first, qg, own, before, cosine, sine):
    rows = heads * BLOCK_Q
    return call(
        functools.partial(attend_body, heads),
        (
            jax.ShapeDtypeStruct((QUARTER, 2 * heads * HEAD), jnp.bfloat16),
            jax.ShapeDtypeStruct((2 * QUARTER, 2 * HEAD), jnp.float32),
        ),
        (begin, first, qg, own, before, cosine, sine),
        [IN_VMEM, IN_SMEM] + [IN_VMEM] * 5,
        heads * 3 * QUARTER * QUARTER * HEAD * 5,
        (
            pltpu.VMEM((2 * QUARTER, HEAD), jnp.bfloat16),
            pltpu.VMEM((2 * QUARTER, HEAD), jnp.bfloat16),
            pltpu.VMEM((rows, HEAD), jnp.bfloat16),
            pltpu.VMEM((rows, HEAD), jnp.bfloat16),
            pltpu.VMEM((SPAN, rows, BLOCK_K), jnp.bfloat16),
            pltpu.VMEM((SPAN, rows, BLOCK_K), jnp.float32),
            pltpu.VMEM((rows, BLOCK_K), jnp.bfloat16),
        ),
    )


def over_groups(field):
    return lax.all_to_all(field, "grp", split_axis=0, concat_axis=0, tiled=True)


def over_plane(field):
    size = lax.axis_size("sp")
    teams = [[low + index for index in range(PARTS)] for low in range(0, size, PARTS)]
    return lax.all_to_all(
        field, "sp", split_axis=0, concat_axis=0, tiled=True, axis_index_groups=teams
    )


def shift(field, step):
    size = lax.axis_size("sp")
    return lax.ppermute(field, "sp", [(index, (index + step) % size) for index in range(size)])


def tables(group_lengths):
    index = lax.axis_index("sp")
    lengths = lax.dynamic_index_in_dim(group_lengths, index % PARTS, 0, keepdims=False)
    base = (index // PARTS - 1) * QUARTER
    rows = base + jnp.arange(2 * QUARTER, dtype=jnp.int32)
    ends = jnp.cumsum(lengths)
    starts = ends - lengths
    begin = jnp.max(jnp.where(rows[:, None] >= starts[None, :], starts[None, :], 0), axis=1)
    half = HEAD // 2
    freq = jnp.power(500000.0, -(2.0 / HEAD) * jnp.arange(half, dtype=jnp.float32))
    angle = (rows - begin).astype(jnp.float32)[:, None] * freq[None, :]
    cosine = jnp.cos(angle)
    sine = jnp.sin(angle)
    begin = begin[QUARTER:] - base
    return (
        jnp.concatenate([cosine, cosine], axis=1),
        jnp.concatenate([-sine, sine], axis=1),
        begin[:, None],
        begin[::BLOCK_Q] // BLOCK_K,
    )


def shards(queries, keys, values, out_grad, dest_group, dest_slot, group_lengths):
    planes = lax.axis_size("grp")
    n_shared = keys.shape[1] // HEAD
    heads = queries.shape[1] // HEAD // planes
    per = heads // CHUNKS

    def by_kv_head(field):
        split = jnp.transpose(field.reshape(TOK, n_shared, HEAD), (1, 0, 2))
        return jnp.repeat(split, planes // n_shared, axis=0)

    note = jnp.concatenate([dest_group, dest_slot]).astype(jnp.bfloat16)
    note = jnp.broadcast_to(note[None, None, :], (planes, 16, 2 * HEAD))
    kv_sent = jnp.concatenate(
        [jnp.concatenate([by_kv_head(keys), by_kv_head(values)], axis=2), note], axis=1
    )
    q_split = queries.reshape(TOK, planes, CHUNKS, per * HEAD)
    g_split = out_grad.reshape(TOK, planes, CHUNKS, per * HEAD)
    kv_here = over_groups(kv_sent)
    qg_here = []
    for chunk in range(CHUNKS):
        joined = jnp.concatenate([q_split[:, :, chunk], g_split[:, :, chunk]], axis=2)
        qg_here.append(over_groups(jnp.transpose(joined, (1, 0, 2))))
    cosine, sine, begin, first = tables(group_lengths)
    code = kv_here[:, TOK, :].astype(jnp.int32)
    code = code[:, :TOK] * TOK + code[:, TOK:]
    code_columns = jnp.transpose(code)
    own = over_plane(place(code, kv_here)).reshape(QUARTER, 2 * HEAD)
    before = shift(own, PARTS)
    home = []
    dkv = None
    for chunk in range(CHUNKS):
        qg = over_plane(place(code, qg_here[chunk])).reshape(QUARTER, 2 * per * HEAD)
        og, dkv_part = attend(per, begin, first, qg, own, before, cosine, sine)
        dkv = dkv_part if dkv is None else dkv + dkv_part
        og = over_plane(og.reshape(PARTS, TOK, 2 * per * HEAD))
        home.append(over_groups(unplace(code_columns, og)))
    spilled = shift(dkv[:QUARTER].astype(jnp.bfloat16), -PARTS)
    dkv = (dkv[QUARTER:] + spilled.astype(jnp.float32)).astype(jnp.bfloat16)
    dkv = over_plane(dkv.reshape(PARTS, TOK, 2 * HEAD))
    dkv = over_groups(unplace(code_columns, dkv)).astype(jnp.float32)
    dkv = jnp.sum(dkv.reshape(n_shared, planes // n_shared, TOK, 2 * HEAD), axis=1)
    dkv = jnp.transpose(dkv.astype(jnp.bfloat16), (1, 0, 2))

    def join(part):
        width = per * HEAD
        pieces = [item[:, :, part * width : (part + 1) * width] for item in home]
        return jnp.transpose(jnp.concatenate(pieces, axis=2), (1, 0, 2)).reshape(TOK, -1)

    return (
        join(0),
        join(1),
        dkv[:, :, :HEAD].reshape(TOK, -1),
        dkv[:, :, HEAD:].reshape(TOK, -1),
    )


def solution(mesh):
    rows = P(("grp", "sp"), None)
    flat = P(("grp", "sp"))
    return jax.shard_map(
        shards,
        mesh=mesh,
        in_specs=(rows, rows, rows, rows, flat, flat, P()),
        out_specs=(rows, rows, rows, rows),
        check_vma=False,
    )
```

```python
import functools
import math

import jax
import jax.numpy as jnp
from jax import lax
from jax.experimental import pallas as pl
from jax.experimental.pallas import tpu as pltpu
from jax.sharding import PartitionSpec as P

HEAD = 128
TOK = 128
PARTS = 8
QUARTER = PARTS * TOK
BLOCK_Q = 256
BLOCK_K = 256
SPAN = QUARTER // BLOCK_K + 1
LOG2E = 1.0 / math.log(2.0)
CHUNKS = 2
SP_IN = (True, True, False)
SP_OUT = (True, True, True)
Z_OUT = (False, False, True)
ATTEND_FLOPS = 8 * 10**9
VMEM = 48 * 1024 * 1024
PACK_VMEM = 60 * 1024 * 1024


def dot(left, right, left_dim, right_dim):
    return lax.dot_general(
        left, right, (((left_dim,), (right_dim,)), ((), ())), preferred_element_type=jnp.float32
    )


def call(body, out_shape, args, specs, flops, scratch=()):
    return pl.pallas_call(
        body,
        out_shape=out_shape,
        in_specs=specs,
        out_specs=jax.tree.map(lambda _: pl.BlockSpec(memory_space=pltpu.VMEM), out_shape),
        scratch_shapes=scratch,
        compiler_params=pltpu.CompilerParams(vmem_limit_bytes=VMEM),
        cost_estimate=pl.CostEstimate(flops=flops, bytes_accessed=4 << 20, transcendentals=0),
    )(*args)


IN_VMEM = pl.BlockSpec(memory_space=pltpu.VMEM)
IN_SMEM = pl.BlockSpec(memory_space=pltpu.SMEM)
UNTOUCHED = pl.BlockSpec(memory_space=pl.ANY)


def flat(field):
    return list(field) if isinstance(field, (list, tuple)) else [field]


def in_ring(base, step):
    return lax.rem(base + (step + PARTS), PARTS)


def view(refs, base, sign, rotated=None):
    if rotated is None:
        rotated = len(refs) > 1
    blocks = refs if len(refs) > 1 else [refs[0].at[step] for step in range(PARTS)]
    return [
        (in_ring(base, sign * step) if rotated else step, block)
        for step, block in enumerate(blocks)
    ]


def rows_of(owner, half=0):
    if isinstance(owner, int):
        return pl.ds(half * QUARTER + owner * TOK, TOK)
    return pl.ds(pl.multiple_of(half * QUARTER + owner * TOK, TOK), TOK)


def columns_of(owner, width, offset=0):
    if isinstance(owner, int):
        return pl.ds(owner * width + offset, width)
    return pl.ds(pl.multiple_of(owner * width + offset, HEAD), width)


def shapes_of(ring, rows, width, kind=jnp.bfloat16):
    if ring:
        return [jax.ShapeDtypeStruct((rows, width), kind)] * PARTS
    return [jax.ShapeDtypeStruct((PARTS, rows, width), kind)]


def cut(refs, *counts):
    parts = []
    for count in counts:
        parts.append(refs[:count])
        refs = refs[count:]
    return parts + [refs]


def count_of(ring):
    return PARTS if ring else 1


def unwrap(outs):
    return list(outs) if len(outs) > 1 else outs[0]


def pack_body(q_hbm, g_hbm, k_hbm, v_hbm, note_hbm, *refs):
    *chunks, sem = refs
    width = chunks[0].shape[2] // 2
    half = TOK // 2
    copies = []
    for chunk, out in enumerate(chunks):
        for plane in range(PARTS):
            columns = pl.ds((plane * CHUNKS + chunk) * width, width)
            copies.append((q_hbm.at[:, columns], out.at[plane, pl.ds(0, TOK), pl.ds(0, width)]))
            copies.append((g_hbm.at[:, columns], out.at[plane, pl.ds(0, TOK), pl.ds(width, width)]))
            if chunk == 0:
                columns = pl.ds(plane // 2 * HEAD, HEAD)
                for part in range(2):
                    rows = pl.ds(part * half, half)
                    for index, field in enumerate((k_hbm, v_hbm)):
                        there = pl.ds((2 * part + index) * HEAD, HEAD)
                        copies.append(
                            (field.at[rows, columns], out.at[plane, pl.ds(TOK, half), there])
                        )
                copies.append((note_hbm, out.at[plane, pl.ds(TOK + half, 16), :]))
    copies = [
        pltpu.make_async_copy(source, target, sem.at[index])
        for index, (source, target) in enumerate(copies)
    ]
    for copy in copies:
        copy.start()
    for copy in copies:
        copy.wait()


def pack(queries, out_grad, keys, values, note):
    width = 2 * queries.shape[1] // PARTS // CHUNKS
    shapes = [
        jax.ShapeDtypeStruct((PARTS, TOK + (TOK // 2 + 16 if chunk == 0 else 0), width), jnp.bfloat16)
        for chunk in range(CHUNKS)
    ]
    return pl.pallas_call(
        pack_body,
        out_shape=shapes,
        in_specs=[UNTOUCHED] * 5,
        out_specs=[IN_VMEM] * CHUNKS,
        scratch_shapes=[pltpu.SemaphoreType.DMA((PARTS * (2 * CHUNKS + 5),))],
        compiler_params=pltpu.CompilerParams(vmem_limit_bytes=PACK_VMEM),
        cost_estimate=pl.CostEstimate(flops=1 << 20, bytes_accessed=4 << 20, transcendentals=0),
    )(queries, out_grad, keys, values, note)


def hot_rows(code_rows, group):
    slots = lax.broadcasted_iota(jnp.int32, (TOK, TOK), 0) + group * TOK
    return jnp.concatenate(
        [jnp.where(slots == row, 1.0, 0.0) for row in code_rows], axis=1
    ).astype(jnp.bfloat16)


def place_first_body(spot_ref, x_ref, _, *refs):
    pairs, outs, (code_ref,) = cut(refs, count_of(SP_IN[0]), count_of(SP_IN[1]))
    half = TOK // 2
    code_rows = []
    for source in range(PARTS):
        note = x_ref[source, TOK + half : TOK + half + 16, :].astype(jnp.float32)
        note = note[:1].astype(jnp.int32)
        code_rows.append(note[:, :TOK] * TOK + note[:, TOK : 2 * TOK])
        code_ref[source : source + 1, :] = code_rows[-1]
    pair_rows = jnp.concatenate(
        [
            x_ref[source, TOK : TOK + half, 2 * HEAD * part : 2 * HEAD * (part + 1)]
            for source in range(PARTS)
            for part in range(2)
        ],
        axis=0,
    )
    rows = x_ref[:, :TOK, :].reshape(QUARTER, x_ref.shape[2])
    for owner, block in view(pairs, spot_ref[1], 1):
        block[...] = dot(hot_rows(code_rows, owner), pair_rows, 1, 0).astype(jnp.bfloat16)
    for owner, block in view(outs, spot_ref[1], 1):
        block[...] = dot(hot_rows(code_rows, owner), rows, 1, 0).astype(jnp.bfloat16)


def place_first(spot, field, after):
    width = field.shape[2]
    outs = call(
        place_first_body,
        shapes_of(SP_IN[0], TOK, 2 * HEAD)
        + shapes_of(SP_IN[1], TOK, width)
        + [jax.ShapeDtypeStruct((PARTS, TOK), jnp.int32)],
        (spot, field, after),
        [IN_SMEM, IN_VMEM, UNTOUCHED],
        2 * QUARTER * QUARTER * (2 * HEAD + width),
    )
    pairs, chunk, (code,) = cut(outs, count_of(SP_IN[0]), count_of(SP_IN[1]))
    return unwrap(pairs), unwrap(chunk), code


def place_body(count, after, spot_ref, code_ref, *refs):
    refs, _, outs = cut(refs, count, after)
    blocks = view(refs, spot_ref[0], -1)
    rows = jnp.concatenate([block[...] for _, block in blocks], axis=0)
    code_rows = [code_ref[pl.ds(owner, 1), :] for owner, _ in blocks]
    for owner, block in view(outs, spot_ref[1], 1):
        hot = hot_rows(code_rows, owner)
        block[...] = dot(hot, rows, 1, 0).astype(jnp.bfloat16)


def place(spot, code, field, ring, after=()):
    field = flat(field)
    width = field[0].shape[-1]
    return unwrap(
        call(
            functools.partial(place_body, len(field), len(after)),
            shapes_of(ring, TOK, width),
            (spot, code, *field, *after),
            [IN_SMEM] + [IN_VMEM] * (1 + len(field)) + [UNTOUCHED] * len(after),
            2 * QUARTER * QUARTER * width,
        )
    )


def unplace_body(count, after, spot_ref, code_ref, *refs):
    main, _, outs = cut(refs, count, after)
    blocks = view(main, spot_ref[1], -1)
    lane = lax.broadcasted_iota(jnp.int32, (1, TOK), 1)
    spots = jnp.concatenate([lane + owner * TOK for owner, _ in blocks], axis=1)
    rows = jnp.concatenate([block[...] for _, block in blocks], axis=0)
    for owner, block in view(outs, spot_ref[0], 1):
        hot = jnp.where(code_ref[owner] == spots, 1.0, 0.0).astype(jnp.bfloat16)
        block[...] = dot(hot, rows, 1, 0).astype(jnp.bfloat16)


def unplace(spot, code_columns, ring, main, after=()):
    main = flat(main)
    width = main[0].shape[-1]
    return unwrap(
        call(
            functools.partial(unplace_body, len(main), len(after)),
            shapes_of(ring, TOK, width),
            (spot, code_columns, *main, *after),
            [IN_SMEM] + [IN_VMEM] * (1 + len(main)) + [UNTOUCHED] * len(after),
            2 * QUARTER * QUARTER * width,
        )
    )


def finish_body(counts, spot_ref, *refs):
    *homes, pairs, (out_ref, q_ref, k_ref, v_ref, pair_ref) = cut(refs, *counts)
    for chunk, home in enumerate(homes):
        for owner, block in view(home, spot_ref[0], -1):
            width = block.shape[1] // 2
            columns = columns_of(owner * CHUNKS + chunk, width)
            out_ref[:, columns] = block[:, :width]
            q_ref[:, columns] = block[:, width:]
    for owner, block in view(pairs, spot_ref[0], -1):
        pair_ref[owner] = block[...]
    for head in range(PARTS // 2):
        columns = pl.ds(head * HEAD, HEAD)
        pair = pair_ref[2 * head].astype(jnp.float32) + pair_ref[2 * head + 1].astype(jnp.float32)
        k_ref[:, columns] = pair[:, :HEAD].astype(jnp.bfloat16)
        v_ref[:, columns] = pair[:, HEAD:].astype(jnp.bfloat16)


def finish(spot, homes, wide, narrow):
    homes = [flat(home) for home in homes]
    args = [block for home in homes for block in home]
    return call(
        functools.partial(finish_body, [len(home) for home in homes]),
        [
            jax.ShapeDtypeStruct((TOK, width), jnp.bfloat16)
            for width in (wide, wide, narrow, narrow)
        ],
        (spot, *args),
        [IN_SMEM] + [IN_VMEM] * len(args),
        1 << 20,
        (pltpu.VMEM((PARTS, TOK, 2 * HEAD), jnp.bfloat16),),
    )


def settle_body(spot_ref, own_ref, spilled_ref, _, *outs):
    for owner, block in view(outs, spot_ref[1], 1):
        at = rows_of(owner)
        block[...] = (own_ref[at, :] + spilled_ref[at, :].astype(jnp.float32)).astype(jnp.bfloat16)


def settle(spot, own, spilled, after):
    return unwrap(
        call(
            settle_body,
            shapes_of(SP_OUT[-1], TOK, 2 * HEAD),
            (spot, own, spilled, after),
            [IN_SMEM, IN_VMEM, IN_VMEM, UNTOUCHED],
            1 << 20,
        )
    )


def wide_tables(table):
    left = lax.broadcasted_iota(jnp.int32, table.shape, 1) < HEAD // 2
    other = pltpu.roll(table, HEAD // 2, 1)
    return jnp.where(left, table, other), jnp.where(left, -other, table)


def turn(field, cosine, sine):
    return field * cosine + pltpu.roll(field, HEAD // 2, 1) * sine


def ready_body(spot_ref, own_ref, before_ref, table_ref, k_ref, v_ref):
    for half, source in ((0, before_ref), (1, own_ref)):
        for owner, block in view([source], spot_ref[1], -1, rotated=SP_IN[0]):
            at = rows_of(owner, half)
            cosine, sine = wide_tables(table_ref[at, :])
            k_ref[at, :] = turn(block[:, :HEAD].astype(jnp.float32), cosine, sine).astype(
                jnp.bfloat16
            )
            v_ref[at, :] = block[:, HEAD:]


def ready(spot, own, before, table):
    return call(
        ready_body,
        [jax.ShapeDtypeStruct((2 * QUARTER, HEAD), jnp.bfloat16)] * 2,
        (spot, own, before, table),
        [IN_SMEM] + [IN_VMEM] * 3,
        1 << 20,
    )


def attend_body(heads, last, count, after, ring, spot_ref, starts_ref, k_hbm, v_hbm, table_hbm, *refs):
    scale = 1.0 / math.sqrt(HEAD)
    rows = heads * BLOCK_Q
    blocks, old_refs, _, outs, sums, refs = cut(
        refs, count, 1 if last else 0, after, count_of(ring), 1
    )
    qg_ref, og_ref, dkv_ref, k_rot, v_all, table_ref, q_rot, g_all, q_turned, g_turned, s_ref, sem = refs
    team = spot_ref[1]
    pairs = [(block, qg_ref.at[rows_of(owner), :]) for owner, block in view(blocks, team, -1)]
    pairs += [(k_hbm, k_rot), (v_hbm, v_all)]
    pairs.append((table_hbm.at[pl.ds(QUARTER, QUARTER), :], table_ref))
    if last:
        pairs.append((old_refs[0], dkv_ref))
    copies = [
        pltpu.make_async_copy(source, target, sem.at[index])
        for index, (source, target) in enumerate(pairs)
    ]
    for copy in copies:
        copy.start()
    if not last:
        dkv_ref[...] = jnp.zeros_like(dkv_ref)
    for copy in copies:
        copy.wait()

    def attend_block(size, low, start, end, cosine, sine):
        here = pl.ds(low, BLOCK_Q)
        wide = size * BLOCK_K
        window = pl.ds(pl.multiple_of(low + (SPAN - size) * BLOCK_K, BLOCK_K), wide)
        q_turned[...] = jnp.transpose(q_rot[...])
        g_turned[...] = jnp.transpose(g_all[...])
        key = lax.broadcasted_iota(jnp.int32, (BLOCK_Q, wide), 1) + (low + (SPAN - size) * BLOCK_K)
        allowed = (key >= start) & (key <= end)
        score = dot(q_rot[...], k_rot[window, :], 1, 1)
        score = jnp.where(
            allowed[None], score.reshape(heads, BLOCK_Q, wide), -jnp.inf
        ).reshape(rows, wide)
        top = jnp.max(score, axis=1, keepdims=True)
        weight = jnp.exp2((score - top) * (scale * LOG2E))
        inverse = 1.0 / jnp.sum(weight, axis=1, keepdims=True)
        weight = weight * inverse
        s_ref[:, :wide] = weight
        mixed = dot(weight.astype(jnp.bfloat16), v_all[window, :], 1, 0)
        delta = jnp.sum(g_all[...].astype(jnp.float32) * mixed, axis=1, keepdims=True)
        weight = s_ref[:, :wide]
        weight_grad = dot(g_all[...], v_all[window, :], 1, 1)
        dkv_ref[HEAD:, window] += dot(g_turned[...], weight.astype(jnp.bfloat16), 1, 0)
        score_grad = (weight * (weight_grad - delta)).astype(jnp.bfloat16)
        dkv_ref[:HEAD, window] += dot(q_turned[...], score_grad, 1, 0)
        q_grad = dot(score_grad, k_rot[window, :], 1, 0)
        for head in range(heads):
            at = slice(head * BLOCK_Q, (head + 1) * BLOCK_Q)
            og_ref[here, pl.ds(head * HEAD, HEAD)] = mixed[at].astype(jnp.bfloat16)
            og_ref[here, pl.ds((heads + head) * HEAD, HEAD)] = turn(
                q_grad[at] * scale, cosine, -sine
            ).astype(jnp.bfloat16)

    @pl.loop(0, QUARTER // BLOCK_Q)
    def _(block):
        low = pl.multiple_of(block * BLOCK_Q, BLOCK_Q)
        here = pl.ds(low, BLOCK_Q)
        cosine, sine = wide_tables(table_ref[here, :])
        for head in range(heads):
            at = pl.ds(head * BLOCK_Q, BLOCK_Q)
            query = qg_ref[here, pl.ds(head * HEAD, HEAD)].astype(jnp.float32)
            q_rot[at, :] = turn(query, cosine, sine).astype(jnp.bfloat16)
            g_all[at, :] = qg_ref[here, pl.ds((heads + head) * HEAD, HEAD)]
        end = lax.broadcasted_iota(jnp.int32, (BLOCK_Q, 1), 0) + (QUARTER + low)
        start = jnp.zeros((BLOCK_Q, 1), jnp.int32)
        first = 0
        for index in range(starts_ref.shape[0]):
            begin = starts_ref[index]
            start = jnp.where(end >= begin, begin, start)
            first = jnp.where(QUARTER + low >= begin, begin, first)
        count = (QUARTER + low + BLOCK_Q - first + BLOCK_K - 1) // BLOCK_K
        q_turned[...] = jnp.transpose(q_rot[...])
        g_turned[...] = jnp.transpose(g_all[...])
        for size in range(1, SPAN + 1):
            pl.when(count == size)(functools.partial(attend_block, size, low, start, end, cosine, sine))

    pairs = [(og_ref.at[rows_of(owner), :], block) for owner, block in view(outs, team, 1)]
    pairs.append((dkv_ref, sums[0]))
    copies = [
        pltpu.make_async_copy(source, target, sem.at[index])
        for index, (source, target) in enumerate(pairs)
    ]
    for copy in copies:
        copy.start()
    for copy in copies:
        copy.wait()


def attend(heads, ring, spot, starts, keys, values, table, blocks, old, after=()):
    rows = heads * BLOCK_Q
    last = old is not None
    wide = 2 * heads * HEAD
    blocks = flat(blocks)
    sums = [jax.ShapeDtypeStruct((2 * HEAD, 2 * QUARTER), jnp.float32)]
    args = [spot, starts, keys, values, table, *blocks] + ([old] if last else [])
    shapes = shapes_of(ring, TOK, wide) + sums
    outs = pl.pallas_call(
        functools.partial(attend_body, heads, last, len(blocks), len(after), ring),
        out_shape=shapes,
        in_specs=[IN_SMEM, IN_SMEM] + [UNTOUCHED] * (len(args) - 2 + len(after)),
        out_specs=[UNTOUCHED] * len(shapes),
        scratch_shapes=(
            pltpu.VMEM((QUARTER, wide), jnp.bfloat16),
            pltpu.VMEM((QUARTER, wide), jnp.bfloat16),
            pltpu.VMEM((2 * HEAD, 2 * QUARTER), jnp.float32),
            pltpu.VMEM((2 * QUARTER, HEAD), jnp.bfloat16),
            pltpu.VMEM((2 * QUARTER, HEAD), jnp.bfloat16),
            pltpu.VMEM((QUARTER, HEAD), jnp.float32),
            pltpu.VMEM((rows, HEAD), jnp.bfloat16),
            pltpu.VMEM((rows, HEAD), jnp.bfloat16),
            pltpu.VMEM((HEAD, rows), jnp.bfloat16),
            pltpu.VMEM((HEAD, rows), jnp.bfloat16),
            pltpu.VMEM((rows, SPAN * BLOCK_K), jnp.float32),
            pltpu.SemaphoreType.DMA((PARTS + 6,)),
        ),
        compiler_params=pltpu.CompilerParams(vmem_limit_bytes=VMEM),
        cost_estimate=pl.CostEstimate(
            flops=ATTEND_FLOPS * heads, bytes_accessed=4 << 20, transcendentals=0
        ),
    )(*args, *after)
    blocks, sums = cut(outs, count_of(ring))
    return unwrap(blocks), sums[0]


def spill_body(sum_ref, table_ref, _, spill_ref, keep_ref):
    scale = 1.0 / math.sqrt(HEAD)
    sums = jnp.transpose(sum_ref[...])
    cosine, sine = wide_tables(table_ref[...])
    turned = turn(sums[:, :HEAD] * scale, cosine, -sine)
    spill_ref[:, :HEAD] = turned[:QUARTER].astype(jnp.bfloat16)
    spill_ref[:, HEAD:] = sums[:QUARTER, HEAD:].astype(jnp.bfloat16)
    keep_ref[:, :HEAD] = turned[QUARTER:]
    keep_ref[:, HEAD:] = sums[QUARTER:, HEAD:]


def spill(sums, table, after):
    return call(
        spill_body,
        [
            jax.ShapeDtypeStruct((QUARTER, 2 * HEAD), jnp.bfloat16),
            jax.ShapeDtypeStruct((QUARTER, 2 * HEAD), jnp.float32),
        ],
        (sums, table, after),
        [IN_VMEM, IN_VMEM, UNTOUCHED],
        1 << 20,
    )


def exchange(field, axis):
    size = lax.axis_size(axis)
    if not isinstance(field, list):
        teams = [[low + index for index in range(PARTS)] for low in range(0, size, PARTS)]
        return lax.all_to_all(
            field, axis, split_axis=0, concat_axis=0, tiled=True, axis_index_groups=teams
        )
    got = [field[0]]
    for step in range(1, PARTS):
        pairs = [
            (index, index - index % PARTS + (index % PARTS + step) % PARTS) for index in range(size)
        ]
        got.append(lax.ppermute(field[step], axis, pairs))
    return got


def shift(field, step):
    size = lax.axis_size("sp")
    return lax.ppermute(field, "sp", [(index, (index + step) % size) for index in range(size)])


def tables(group_lengths):
    index = lax.axis_index("sp")
    lengths = lax.dynamic_index_in_dim(group_lengths, index % PARTS, 0, keepdims=False)
    starts = jnp.cumsum(lengths) - lengths - (index // PARTS - 1) * QUARTER
    rows = jnp.arange(2 * QUARTER, dtype=jnp.int32)[:, None]
    begin = jnp.max(jnp.where(rows >= starts[None, :], starts[None, :], -QUARTER), axis=1)
    position = rows[:, 0] - jnp.maximum(begin, -QUARTER)
    freq = jnp.power(500000.0, -(2.0 / HEAD) * jnp.arange(HEAD // 2, dtype=jnp.float32))
    angle = position.astype(jnp.float32)[:, None] * freq[None, :]
    return starts, jnp.concatenate([jnp.cos(angle), jnp.sin(angle)], axis=1)


def shards(queries, keys, values, out_grad, dest_group, dest_slot, group_lengths):
    heads = queries.shape[1] // HEAD // lax.axis_size("grp") // CHUNKS
    spot = jnp.stack([lax.axis_index("grp"), lax.axis_index("sp") % PARTS]).astype(jnp.int32)
    note = jnp.concatenate([dest_group, dest_slot]).astype(jnp.bfloat16)
    note = jnp.broadcast_to(jnp.concatenate([note, note])[None, :], (16, 4 * HEAD))
    first, second = [
        exchange(chunk, "grp") for chunk in pack(queries, out_grad, keys, values, note)
    ]
    starts, table = tables(group_lengths)
    pairs, first, code = place_first(spot, first, table)
    code_columns = code[:, :, None]
    pairs = exchange(pairs, "sp")
    first = exchange(first, "sp")
    own = jnp.stack(pairs) if isinstance(pairs, list) else pairs
    before = shift(own, PARTS)
    k_rot, v_all = ready(spot, own, before, table)
    fixed = (spot, starts, k_rot, v_all, table)
    second = place(spot, code, second, SP_IN[2])
    blocks, sums = attend(heads, SP_OUT[0], *fixed, first, None)
    early = unplace(
        spot, code_columns, Z_OUT[0], exchange(blocks, "sp"), after=flat(second)[:1]
    )
    blocks, sums = attend(
        heads, SP_OUT[1], *fixed, exchange(second, "sp"), sums, after=flat(early)[:1] if SP_OUT[0] else ()
    )
    early_home = exchange(early, "grp")
    spilled, keep = spill(sums, table, flat(early)[0])
    spilled = shift(spilled, -PARTS)
    blocks = exchange(blocks, "sp")
    pairs = settle(spot, keep, spilled, flat(blocks)[-1])
    late = unplace(
        spot, code_columns, Z_OUT[1], blocks, after=flat(early)[:1] + flat(pairs)[:1]
    )
    pairs = unplace(spot, code_columns, Z_OUT[2], exchange(pairs, "sp"))
    homes = [early_home, exchange(late, "grp"), exchange(pairs, "grp")]
    return tuple(finish(spot, homes, queries.shape[1], keys.shape[1]))


def solution(mesh):
    rows = P(("grp", "sp"), None)
    flat = P(("grp", "sp"))
    return jax.shard_map(
        shards,
        mesh=mesh,
        in_specs=(rows, rows, rows, rows, flat, flat, P()),
        out_specs=(rows, rows, rows, rows),
        check_vma=False,
    )
```

```python
import functools
import math

import jax
import jax.numpy as jnp
from jax import lax
from jax.experimental import pallas as pl
from jax.experimental.pallas import tpu as pltpu
from jax.sharding import PartitionSpec as P

HEAD = 128
TOK = 128
PARTS = 8
QUARTER = PARTS * TOK
BLOCK_Q = 256
BLOCK_K = 256
SPAN = QUARTER // BLOCK_K + 1
LOG2E = 1.0 / math.log(2.0)
CHUNKS = 2
SP_IN = (True, True, False)
SP_OUT = (False, True, True)
Z_OUT = (False, False, True)
PAIRS_FIRST = False
ATTEND_FLOPS = 8 * 10**9
VMEM = 48 * 1024 * 1024
PACK_VMEM = 60 * 1024 * 1024


def dot(left, right, left_dim, right_dim):
    return lax.dot_general(
        left, right, (((left_dim,), (right_dim,)), ((), ())), preferred_element_type=jnp.float32
    )


def call(body, out_shape, args, specs, flops, scratch=()):
    return pl.pallas_call(
        body,
        out_shape=out_shape,
        in_specs=specs,
        out_specs=jax.tree.map(lambda _: pl.BlockSpec(memory_space=pltpu.VMEM), out_shape),
        scratch_shapes=scratch,
        compiler_params=pltpu.CompilerParams(vmem_limit_bytes=VMEM),
        cost_estimate=pl.CostEstimate(flops=flops, bytes_accessed=4 << 20, transcendentals=0),
    )(*args)


IN_VMEM = pl.BlockSpec(memory_space=pltpu.VMEM)
IN_SMEM = pl.BlockSpec(memory_space=pltpu.SMEM)
UNTOUCHED = pl.BlockSpec(memory_space=pl.ANY)


def flat(field):
    return list(field) if isinstance(field, (list, tuple)) else [field]


def in_ring(base, step):
    return lax.rem(base + (step + PARTS), PARTS)


def view(refs, base, sign, rotated=None):
    if rotated is None:
        rotated = len(refs) > 1
    blocks = refs if len(refs) > 1 else [refs[0].at[step] for step in range(PARTS)]
    return [
        (in_ring(base, sign * step) if rotated else step, block)
        for step, block in enumerate(blocks)
    ]


def rows_of(owner, half=0):
    if isinstance(owner, int):
        return pl.ds(half * QUARTER + owner * TOK, TOK)
    return pl.ds(pl.multiple_of(half * QUARTER + owner * TOK, TOK), TOK)


def columns_of(owner, width, offset=0):
    if isinstance(owner, int):
        return pl.ds(owner * width + offset, width)
    return pl.ds(pl.multiple_of(owner * width + offset, HEAD), width)


def shapes_of(ring, rows, width, kind=jnp.bfloat16):
    if ring:
        return [jax.ShapeDtypeStruct((rows, width), kind)] * PARTS
    return [jax.ShapeDtypeStruct((PARTS, rows, width), kind)]


def cut(refs, *counts):
    parts = []
    for count in counts:
        parts.append(refs[:count])
        refs = refs[count:]
    return parts + [refs]


def count_of(ring):
    return PARTS if ring else 1


def unwrap(outs):
    return list(outs) if len(outs) > 1 else outs[0]


def pack_body(chunk, count, q_hbm, g_hbm, *refs):
    extra, (out, sem) = cut(refs, count)
    width = out.shape[2] // 2
    half = TOK // 2
    copies = []
    for plane in range(PARTS):
        columns = pl.ds((plane * CHUNKS + chunk) * width, width)
        copies.append((q_hbm.at[:, columns], out.at[plane, pl.ds(0, TOK), pl.ds(0, width)]))
        copies.append((g_hbm.at[:, columns], out.at[plane, pl.ds(0, TOK), pl.ds(width, width)]))
        if extra:
            k_hbm, v_hbm, note_hbm = extra
            columns = pl.ds(plane // 2 * HEAD, HEAD)
            for part in range(2):
                rows = pl.ds(part * half, half)
                for index, field in enumerate((k_hbm, v_hbm)):
                    there = pl.ds((2 * part + index) * HEAD, HEAD)
                    copies.append((field.at[rows, columns], out.at[plane, pl.ds(TOK, half), there]))
            copies.append((note_hbm, out.at[plane, pl.ds(TOK + half, 16), :]))
    copies = [
        pltpu.make_async_copy(source, target, sem.at[index])
        for index, (source, target) in enumerate(copies)
    ]
    for copy in copies:
        copy.start()
    for copy in copies:
        copy.wait()


def pack(chunk, queries, out_grad, *extra):
    width = 2 * queries.shape[1] // PARTS // CHUNKS
    depth = TOK + (TOK // 2 + 16 if extra else 0)
    return pl.pallas_call(
        functools.partial(pack_body, chunk, len(extra)),
        out_shape=jax.ShapeDtypeStruct((PARTS, depth, width), jnp.bfloat16),
        in_specs=[UNTOUCHED] * (2 + len(extra)),
        out_specs=IN_VMEM,
        scratch_shapes=[pltpu.SemaphoreType.DMA((PARTS * 7,))],
        compiler_params=pltpu.CompilerParams(vmem_limit_bytes=PACK_VMEM),
        cost_estimate=pl.CostEstimate(flops=1 << 20, bytes_accessed=4 << 20, transcendentals=0),
    )(queries, out_grad, *extra)


def hot_rows(code_rows, group):
    slots = lax.broadcasted_iota(jnp.int32, (TOK, TOK), 0) + group * TOK
    return jnp.concatenate(
        [jnp.where(slots == row, 1.0, 0.0) for row in code_rows], axis=1
    ).astype(jnp.bfloat16)


def place_first_body(spot_ref, x_ref, _, __, *refs):
    pairs, outs, (code_ref,) = cut(refs, count_of(SP_IN[0]), count_of(SP_IN[1]))
    half = TOK // 2
    code_rows = []
    for source in range(PARTS):
        note = x_ref[source, TOK + half : TOK + half + 16, :].astype(jnp.float32)
        note = note[:1].astype(jnp.int32)
        code_rows.append(note[:, :TOK] * TOK + note[:, TOK : 2 * TOK])
        code_ref[source : source + 1, :] = code_rows[-1]
    pair_rows = jnp.concatenate(
        [
            x_ref[source, TOK : TOK + half, 2 * HEAD * part : 2 * HEAD * (part + 1)]
            for source in range(PARTS)
            for part in range(2)
        ],
        axis=0,
    )
    rows = x_ref[:, :TOK, :].reshape(QUARTER, x_ref.shape[2])
    for owner, block in view(pairs, spot_ref[1], 1):
        block[...] = dot(hot_rows(code_rows, owner), pair_rows, 1, 0).astype(jnp.bfloat16)
    for owner, block in view(outs, spot_ref[1], 1):
        block[...] = dot(hot_rows(code_rows, owner), rows, 1, 0).astype(jnp.bfloat16)


def place_first(spot, field, *after):
    width = field.shape[2]
    outs = call(
        place_first_body,
        shapes_of(SP_IN[0], TOK, 2 * HEAD)
        + shapes_of(SP_IN[1], TOK, width)
        + [jax.ShapeDtypeStruct((PARTS, TOK), jnp.int32)],
        (spot, field, *after),
        [IN_SMEM, IN_VMEM, UNTOUCHED, UNTOUCHED],
        2 * QUARTER * QUARTER * (2 * HEAD + width),
    )
    pairs, chunk, (code,) = cut(outs, count_of(SP_IN[0]), count_of(SP_IN[1]))
    return unwrap(pairs), unwrap(chunk), code


def place_body(count, after, spot_ref, code_ref, *refs):
    refs, _, outs = cut(refs, count, after)
    blocks = view(refs, spot_ref[0], -1)
    rows = jnp.concatenate([block[...] for _, block in blocks], axis=0)
    code_rows = [code_ref[pl.ds(owner, 1), :] for owner, _ in blocks]
    for owner, block in view(outs, spot_ref[1], 1):
        hot = hot_rows(code_rows, owner)
        block[...] = dot(hot, rows, 1, 0).astype(jnp.bfloat16)


def place(spot, code, field, ring, after=()):
    field = flat(field)
    width = field[0].shape[-1]
    return unwrap(
        call(
            functools.partial(place_body, len(field), len(after)),
            shapes_of(ring, TOK, width),
            (spot, code, *field, *after),
            [IN_SMEM] + [IN_VMEM] * (1 + len(field)) + [UNTOUCHED] * len(after),
            2 * QUARTER * QUARTER * width,
        )
    )


def unplace_body(count, after, spot_ref, code_ref, *refs):
    main, _, outs = cut(refs, count, after)
    blocks = view(main, spot_ref[1], -1)
    lane = lax.broadcasted_iota(jnp.int32, (1, TOK), 1)
    spots = jnp.concatenate([lane + owner * TOK for owner, _ in blocks], axis=1)
    rows = jnp.concatenate([block[...] for _, block in blocks], axis=0)
    for owner, block in view(outs, spot_ref[0], 1):
        hot = jnp.where(code_ref[owner] == spots, 1.0, 0.0).astype(jnp.bfloat16)
        block[...] = dot(hot, rows, 1, 0).astype(jnp.bfloat16)


def unplace(spot, code_columns, ring, main, after=()):
    main = flat(main)
    width = main[0].shape[-1]
    return unwrap(
        call(
            functools.partial(unplace_body, len(main), len(after)),
            shapes_of(ring, TOK, width),
            (spot, code_columns, *main, *after),
            [IN_SMEM] + [IN_VMEM] * (1 + len(main)) + [UNTOUCHED] * len(after),
            2 * QUARTER * QUARTER * width,
        )
    )


def finish_body(counts, spot_ref, *refs):
    *homes, pairs, (out_ref, q_ref, k_ref, v_ref, pair_ref) = cut(refs, *counts)
    for chunk, home in enumerate(homes):
        for owner, block in view(home, spot_ref[0], -1):
            width = block.shape[1] // 2
            columns = columns_of(owner * CHUNKS + chunk, width)
            out_ref[:, columns] = block[:, :width]
            q_ref[:, columns] = block[:, width:]
    for owner, block in view(pairs, spot_ref[0], -1):
        pair_ref[owner] = block[...]
    for head in range(PARTS // 2):
        columns = pl.ds(head * HEAD, HEAD)
        pair = pair_ref[2 * head].astype(jnp.float32) + pair_ref[2 * head + 1].astype(jnp.float32)
        k_ref[:, columns] = pair[:, :HEAD].astype(jnp.bfloat16)
        v_ref[:, columns] = pair[:, HEAD:].astype(jnp.bfloat16)


def finish(spot, homes, wide, narrow):
    homes = [flat(home) for home in homes]
    args = [block for home in homes for block in home]
    return call(
        functools.partial(finish_body, [len(home) for home in homes]),
        [
            jax.ShapeDtypeStruct((TOK, width), jnp.bfloat16)
            for width in (wide, wide, narrow, narrow)
        ],
        (spot, *args),
        [IN_SMEM] + [IN_VMEM] * len(args),
        1 << 20,
        (pltpu.VMEM((PARTS, TOK, 2 * HEAD), jnp.bfloat16),),
    )


def settle_body(after, spot_ref, own_ref, spilled_ref, *refs):
    _, outs = cut(refs, after)
    for owner, block in view(outs, spot_ref[1], 1):
        at = rows_of(owner)
        block[...] = (own_ref[at, :] + spilled_ref[at, :].astype(jnp.float32)).astype(jnp.bfloat16)


def settle(spot, own, spilled, after):
    return unwrap(
        call(
            functools.partial(settle_body, len(after)),
            shapes_of(SP_OUT[-1], TOK, 2 * HEAD),
            (spot, own, spilled, *after),
            [IN_SMEM, IN_VMEM, IN_VMEM] + [UNTOUCHED] * len(after),
            1 << 20,
        )
    )


def wide_tables(table):
    left = lax.broadcasted_iota(jnp.int32, table.shape, 1) < HEAD // 2
    other = pltpu.roll(table, HEAD // 2, 1)
    return jnp.where(left, table, other), jnp.where(left, -other, table)


def turn(field, cosine, sine):
    return field * cosine + pltpu.roll(field, HEAD // 2, 1) * sine


def ready_body(spot_ref, own_ref, before_ref, table_ref, k_ref, v_ref):
    for half, source in ((0, before_ref), (1, own_ref)):
        for owner, block in view([source], spot_ref[1], -1, rotated=SP_IN[0]):
            at = rows_of(owner, half)
            cosine, sine = wide_tables(table_ref[at, :])
            k_ref[at, :] = turn(block[:, :HEAD].astype(jnp.float32), cosine, sine).astype(
                jnp.bfloat16
            )
            v_ref[at, :] = block[:, HEAD:]


def ready(spot, own, before, table):
    return call(
        ready_body,
        [jax.ShapeDtypeStruct((2 * QUARTER, HEAD), jnp.bfloat16)] * 2,
        (spot, own, before, table),
        [IN_SMEM] + [IN_VMEM] * 3,
        1 << 20,
    )


def attend_body(heads, last, count, after, ring, spot_ref, starts_ref, k_hbm, v_hbm, table_hbm, *refs):
    scale = 1.0 / math.sqrt(HEAD)
    rows = heads * BLOCK_Q
    blocks, old_refs, _, outs, sums, refs = cut(
        refs, count, 1 if last else 0, after, count_of(ring), 1
    )
    qg_ref, og_ref, dkv_ref, k_rot, v_all, table_ref, q_rot, g_all, q_turned, g_turned, s_ref, p_ref, d_ref, sem = refs
    team = spot_ref[1]
    pairs = [(block, qg_ref.at[rows_of(owner), :]) for owner, block in view(blocks, team, -1)]
    pairs += [(k_hbm, k_rot), (v_hbm, v_all)]
    pairs.append((table_hbm.at[pl.ds(QUARTER, QUARTER), :], table_ref))
    if last:
        pairs.append((old_refs[0], dkv_ref))
    copies = [
        pltpu.make_async_copy(source, target, sem.at[index])
        for index, (source, target) in enumerate(pairs)
    ]
    for copy in copies:
        copy.start()
    if not last:
        dkv_ref[...] = jnp.zeros_like(dkv_ref)
    for copy in copies:
        copy.wait()

    def attend_block(size, low, start, end, cosine, sine):
        here = pl.ds(low, BLOCK_Q)
        wide = size * BLOCK_K
        window = pl.ds(pl.multiple_of(low + (SPAN - size) * BLOCK_K, BLOCK_K), wide)
        key = lax.broadcasted_iota(jnp.int32, (BLOCK_Q, wide), 1) + (low + (SPAN - size) * BLOCK_K)
        allowed = (key >= start) & (key <= end)
        for head in range(heads):
            at = pl.ds(head * BLOCK_Q, BLOCK_Q)
            score = jnp.where(allowed, dot(q_rot[at, :], k_rot[window, :], 1, 1), -jnp.inf)
            top = jnp.max(score, axis=1, keepdims=True)
            weight = jnp.exp2((score - top) * (scale * LOG2E))
            weight = weight * (1.0 / jnp.sum(weight, axis=1, keepdims=True))
            weight_low = weight.astype(jnp.bfloat16)
            p_ref[at, :wide] = weight_low
            s_ref[at, :wide] = weight
            mixed = dot(weight_low, v_all[window, :], 1, 0)
            og_ref[here, pl.ds(head * HEAD, HEAD)] = mixed.astype(jnp.bfloat16)
            g_rows = g_all[at, :]
            delta = jnp.sum(g_rows.astype(jnp.float32) * mixed, axis=1, keepdims=True)
            weight_grad = dot(g_rows, v_all[window, :], 1, 1)
            score_grad = (s_ref[at, :wide] * (weight_grad - delta)).astype(jnp.bfloat16)
            d_ref[at, :wide] = score_grad
            q_grad = dot(score_grad, k_rot[window, :], 1, 0)
            dkv_ref[HEAD:, window] += dot(g_turned[:, at], p_ref[at, :wide], 1, 0)
            dkv_ref[:HEAD, window] += dot(q_turned[:, at], d_ref[at, :wide], 1, 0)
            og_ref[here, pl.ds((heads + head) * HEAD, HEAD)] = turn(
                q_grad * scale, cosine, -sine
            ).astype(jnp.bfloat16)

    @pl.loop(0, QUARTER // BLOCK_Q)
    def _(block):
        low = pl.multiple_of(block * BLOCK_Q, BLOCK_Q)
        here = pl.ds(low, BLOCK_Q)
        cosine, sine = wide_tables(table_ref[here, :])
        for head in range(heads):
            at = pl.ds(head * BLOCK_Q, BLOCK_Q)
            query = qg_ref[here, pl.ds(head * HEAD, HEAD)].astype(jnp.float32)
            q_rot[at, :] = turn(query, cosine, sine).astype(jnp.bfloat16)
            g_all[at, :] = qg_ref[here, pl.ds((heads + head) * HEAD, HEAD)]
        end = lax.broadcasted_iota(jnp.int32, (BLOCK_Q, 1), 0) + (QUARTER + low)
        start = jnp.zeros((BLOCK_Q, 1), jnp.int32)
        first = 0
        for index in range(starts_ref.shape[0]):
            begin = starts_ref[index]
            start = jnp.where(end >= begin, begin, start)
            first = jnp.where(QUARTER + low >= begin, begin, first)
        count = (QUARTER + low + BLOCK_Q - first + BLOCK_K - 1) // BLOCK_K
        q_turned[...] = jnp.transpose(q_rot[...])
        g_turned[...] = jnp.transpose(g_all[...])
        for size in range(1, SPAN + 1):
            pl.when(count == size)(functools.partial(attend_block, size, low, start, end, cosine, sine))

    pairs = [(og_ref.at[rows_of(owner), :], block) for owner, block in view(outs, team, 1)]
    pairs.append((dkv_ref, sums[0]))
    copies = [
        pltpu.make_async_copy(source, target, sem.at[index])
        for index, (source, target) in enumerate(pairs)
    ]
    for copy in copies:
        copy.start()
    for copy in copies:
        copy.wait()


def attend(heads, ring, spot, starts, keys, values, table, blocks, old, after=()):
    rows = heads * BLOCK_Q
    last = old is not None
    wide = 2 * heads * HEAD
    blocks = flat(blocks)
    sums = [jax.ShapeDtypeStruct((2 * HEAD, 2 * QUARTER), jnp.float32)]
    args = [spot, starts, keys, values, table, *blocks] + ([old] if last else [])
    shapes = shapes_of(ring, TOK, wide) + sums
    outs = pl.pallas_call(
        functools.partial(attend_body, heads, last, len(blocks), len(after), ring),
        out_shape=shapes,
        in_specs=[IN_SMEM, IN_SMEM] + [UNTOUCHED] * (len(args) - 2 + len(after)),
        out_specs=[UNTOUCHED] * len(shapes),
        scratch_shapes=(
            pltpu.VMEM((QUARTER, wide), jnp.bfloat16),
            pltpu.VMEM((QUARTER, wide), jnp.bfloat16),
            pltpu.VMEM((2 * HEAD, 2 * QUARTER), jnp.float32),
            pltpu.VMEM((2 * QUARTER, HEAD), jnp.bfloat16),
            pltpu.VMEM((2 * QUARTER, HEAD), jnp.bfloat16),
            pltpu.VMEM((QUARTER, HEAD), jnp.float32),
            pltpu.VMEM((rows, HEAD), jnp.bfloat16),
            pltpu.VMEM((rows, HEAD), jnp.bfloat16),
            pltpu.VMEM((HEAD, rows), jnp.bfloat16),
            pltpu.VMEM((HEAD, rows), jnp.bfloat16),
            pltpu.VMEM((rows, SPAN * BLOCK_K), jnp.float32),
            pltpu.VMEM((rows, SPAN * BLOCK_K), jnp.bfloat16),
            pltpu.VMEM((rows, SPAN * BLOCK_K), jnp.bfloat16),
            pltpu.SemaphoreType.DMA((PARTS + 6,)),
        ),
        compiler_params=pltpu.CompilerParams(vmem_limit_bytes=PACK_VMEM),
        cost_estimate=pl.CostEstimate(
            flops=ATTEND_FLOPS * heads, bytes_accessed=4 << 20, transcendentals=0
        ),
    )(*args, *after)
    blocks, sums = cut(outs, count_of(ring))
    return unwrap(blocks), sums[0]


def spill_body(sum_ref, table_ref, _, spill_ref, keep_ref):
    scale = 1.0 / math.sqrt(HEAD)
    sums = jnp.transpose(sum_ref[...])
    cosine, sine = wide_tables(table_ref[...])
    turned = turn(sums[:, :HEAD] * scale, cosine, -sine)
    spill_ref[:, :HEAD] = turned[:QUARTER].astype(jnp.bfloat16)
    spill_ref[:, HEAD:] = sums[:QUARTER, HEAD:].astype(jnp.bfloat16)
    keep_ref[:, :HEAD] = turned[QUARTER:]
    keep_ref[:, HEAD:] = sums[QUARTER:, HEAD:]


def spill(sums, table, after):
    return call(
        spill_body,
        [
            jax.ShapeDtypeStruct((QUARTER, 2 * HEAD), jnp.bfloat16),
            jax.ShapeDtypeStruct((QUARTER, 2 * HEAD), jnp.float32),
        ],
        (sums, table, after),
        [IN_VMEM, IN_VMEM, UNTOUCHED],
        1 << 20,
    )


def tie_body(count, *refs):
    pass


def tie(field, *after):
    parts = flat(field)
    outs = pl.pallas_call(
        functools.partial(tie_body, len(parts)),
        out_shape=[jax.ShapeDtypeStruct(part.shape, part.dtype) for part in parts],
        in_specs=[UNTOUCHED] * (len(parts) + len(after)),
        out_specs=[UNTOUCHED] * len(parts),
        input_output_aliases={index: index for index in range(len(parts))},
        cost_estimate=pl.CostEstimate(flops=1, bytes_accessed=1, transcendentals=0),
    )(*parts, *after)
    return unwrap(list(outs))


def exchange(field, axis):
    size = lax.axis_size(axis)
    if not isinstance(field, list):
        teams = [[low + index for index in range(PARTS)] for low in range(0, size, PARTS)]
        return lax.all_to_all(
            field, axis, split_axis=0, concat_axis=0, tiled=True, axis_index_groups=teams
        )
    got = [field[0]]
    for step in range(1, PARTS):
        pairs = [
            (index, index - index % PARTS + (index % PARTS + step) % PARTS) for index in range(size)
        ]
        got.append(lax.ppermute(field[step], axis, pairs))
    return got


def shift(field, step):
    size = lax.axis_size("sp")
    return lax.ppermute(field, "sp", [(index, (index + step) % size) for index in range(size)])


def tables(group_lengths):
    index = lax.axis_index("sp")
    lengths = lax.dynamic_index_in_dim(group_lengths, index % PARTS, 0, keepdims=False)
    starts = jnp.cumsum(lengths) - lengths - (index // PARTS - 1) * QUARTER
    rows = jnp.arange(2 * QUARTER, dtype=jnp.int32)[:, None]
    begin = jnp.max(jnp.where(rows >= starts[None, :], starts[None, :], -QUARTER), axis=1)
    position = rows[:, 0] - jnp.maximum(begin, -QUARTER)
    freq = jnp.power(500000.0, -(2.0 / HEAD) * jnp.arange(HEAD // 2, dtype=jnp.float32))
    angle = position.astype(jnp.float32)[:, None] * freq[None, :]
    return starts, jnp.concatenate([jnp.cos(angle), jnp.sin(angle)], axis=1)


def shards(queries, keys, values, out_grad, dest_group, dest_slot, group_lengths):
    heads = queries.shape[1] // HEAD // lax.axis_size("grp") // CHUNKS
    spot = jnp.stack([lax.axis_index("grp"), lax.axis_index("sp") % PARTS]).astype(jnp.int32)
    note = jnp.concatenate([dest_group, dest_slot]).astype(jnp.bfloat16)
    note = jnp.broadcast_to(jnp.concatenate([note, note])[None, :], (16, 4 * HEAD))
    first = exchange(pack(0, queries, out_grad, keys, values, note), "grp")
    second = exchange(pack(1, queries, out_grad), "grp")
    starts, table = tables(group_lengths)
    pairs, first, code = place_first(spot, first, table, starts)
    code_columns = code[:, :, None]
    pairs = exchange(pairs, "sp")
    first = exchange(first, "sp")
    own = jnp.stack(pairs) if isinstance(pairs, list) else pairs
    before = shift(own, PARTS)
    k_rot, v_all = ready(spot, own, before, table)
    fixed = (spot, starts, k_rot, v_all, table)
    second = place(spot, code, second, SP_IN[2])
    blocks, sums = attend(heads, SP_OUT[0], *fixed, first, None, after=flat(second)[:1])
    second = exchange(second, "sp")
    early = exchange(tie(blocks, flat(second)[-1]), "sp")
    blocks, sums = attend(heads, SP_OUT[1], *fixed, second, sums)
    early = unplace(spot, code_columns, Z_OUT[0], early, after=flat(blocks)[:1])
    early_home = exchange(early, "grp")
    spilled, keep = spill(sums, table, flat(early)[0])
    spilled = shift(spilled, -PARTS)
    blocks = exchange(blocks, "sp")
    pairs = settle(spot, keep, spilled, flat(blocks))
    if PAIRS_FIRST:
        pairs = unplace(spot, code_columns, Z_OUT[2], exchange(pairs, "sp"))
    late = unplace(
        spot, code_columns, Z_OUT[1], blocks, after=flat(early_home)[:1] + flat(pairs)[:1]
    )
    if not PAIRS_FIRST:
        pairs = unplace(spot, code_columns, Z_OUT[2], exchange(pairs, "sp"))
    homes = [early_home, exchange(late, "grp"), exchange(pairs, "grp")]
    return tuple(finish(spot, homes, queries.shape[1], keys.shape[1]))


def solution(mesh):
    rows = P(("grp", "sp"), None)
    flat = P(("grp", "sp"))
    return jax.shard_map(
        shards,
        mesh=mesh,
        in_specs=(rows, rows, rows, rows, flat, flat, P()),
        out_specs=(rows, rows, rows, rows),
        check_vma=False,
    )
```

```python
import functools
import math

import jax
import jax.numpy as jnp
from jax import lax
from jax.experimental import pallas as pl
from jax.experimental.pallas import tpu as pltpu
from jax.sharding import PartitionSpec as P

HEAD = 128
TOK = 128
PARTS = 8
QUARTER = PARTS * TOK
BLOCK_Q = 256
BLOCK_K = 256
SPAN = QUARTER // BLOCK_K + 1
LOG2E = 1.0 / math.log(2.0)
CHUNKS = 2
SP_IN = (True, False)
SP_OUT = (False, True, True)
Z_OUT = (False, False, True)
PAIRS_FIRST = False
ATTEND_FLOPS = 8 * 10**9
VMEM = 48 * 1024 * 1024
PACK_VMEM = 60 * 1024 * 1024


def dot(left, right, left_dim, right_dim):
    return lax.dot_general(
        left, right, (((left_dim,), (right_dim,)), ((), ())), preferred_element_type=jnp.float32
    )


def call(body, out_shape, args, specs, flops, scratch=()):
    return pl.pallas_call(
        body,
        out_shape=out_shape,
        in_specs=specs,
        out_specs=jax.tree.map(lambda _: pl.BlockSpec(memory_space=pltpu.VMEM), out_shape),
        scratch_shapes=scratch,
        compiler_params=pltpu.CompilerParams(vmem_limit_bytes=VMEM),
        cost_estimate=pl.CostEstimate(flops=flops, bytes_accessed=4 << 20, transcendentals=0),
    )(*args)


IN_VMEM = pl.BlockSpec(memory_space=pltpu.VMEM)
IN_SMEM = pl.BlockSpec(memory_space=pltpu.SMEM)
UNTOUCHED = pl.BlockSpec(memory_space=pl.ANY)


def flat(field):
    return list(field) if isinstance(field, (list, tuple)) else [field]


def in_ring(base, step):
    return lax.rem(base + (step + PARTS), PARTS)


def view(refs, base, sign, rotated=None):
    if rotated is None:
        rotated = len(refs) > 1
    blocks = refs if len(refs) > 1 else [refs[0].at[step] for step in range(PARTS)]
    return [
        (in_ring(base, sign * step) if rotated else step, block)
        for step, block in enumerate(blocks)
    ]


def rows_of(owner, half=0):
    if isinstance(owner, int):
        return pl.ds(half * QUARTER + owner * TOK, TOK)
    return pl.ds(pl.multiple_of(half * QUARTER + owner * TOK, TOK), TOK)


def columns_of(owner, width, offset=0):
    if isinstance(owner, int):
        return pl.ds(owner * width + offset, width)
    return pl.ds(pl.multiple_of(owner * width + offset, HEAD), width)


def shapes_of(ring, rows, width, kind=jnp.bfloat16):
    if ring:
        return [jax.ShapeDtypeStruct((rows, width), kind)] * PARTS
    return [jax.ShapeDtypeStruct((PARTS, rows, width), kind)]


def cut(refs, *counts):
    parts = []
    for count in counts:
        parts.append(refs[:count])
        refs = refs[count:]
    return parts + [refs]


def count_of(ring):
    return PARTS if ring else 1


def unwrap(outs):
    return list(outs) if len(outs) > 1 else outs[0]


def pack_body(chunk, count, q_hbm, g_hbm, *refs):
    extra, (out, sem) = cut(refs, count)
    width = out.shape[2] // 2
    half = TOK // 2
    copies = []
    for plane in range(PARTS):
        columns = pl.ds((plane * CHUNKS + chunk) * width, width)
        copies.append((q_hbm.at[:, columns], out.at[plane, pl.ds(0, TOK), pl.ds(0, width)]))
        copies.append((g_hbm.at[:, columns], out.at[plane, pl.ds(0, TOK), pl.ds(width, width)]))
        if extra:
            k_hbm, v_hbm, note_hbm = extra
            columns = pl.ds(plane // 2 * HEAD, HEAD)
            for part in range(2):
                rows = pl.ds(part * half, half)
                for index, field in enumerate((k_hbm, v_hbm)):
                    there = pl.ds((2 * part + index) * HEAD, HEAD)
                    copies.append((field.at[rows, columns], out.at[plane, pl.ds(TOK, half), there]))
            copies.append((note_hbm, out.at[plane, pl.ds(TOK + half, 16), :]))
    copies = [
        pltpu.make_async_copy(source, target, sem.at[index])
        for index, (source, target) in enumerate(copies)
    ]
    for copy in copies:
        copy.start()
    for copy in copies:
        copy.wait()


def pack(chunk, queries, out_grad, *extra):
    width = 2 * queries.shape[1] // PARTS // CHUNKS
    depth = TOK + (TOK // 2 + 16 if extra else 0)
    return pl.pallas_call(
        functools.partial(pack_body, chunk, len(extra)),
        out_shape=jax.ShapeDtypeStruct((PARTS, depth, width), jnp.bfloat16),
        in_specs=[UNTOUCHED] * (2 + len(extra)),
        out_specs=IN_VMEM,
        scratch_shapes=[pltpu.SemaphoreType.DMA((PARTS * 7,))],
        compiler_params=pltpu.CompilerParams(vmem_limit_bytes=PACK_VMEM),
        cost_estimate=pl.CostEstimate(flops=1 << 20, bytes_accessed=4 << 20, transcendentals=0),
    )(queries, out_grad, *extra)


def hot_rows(code_rows, group):
    slots = lax.broadcasted_iota(jnp.int32, (TOK, TOK), 0) + group * TOK
    return jnp.concatenate(
        [jnp.where(slots == row, 1.0, 0.0) for row in code_rows], axis=1
    ).astype(jnp.bfloat16)


def place_first_body(spot_ref, x_ref, _, __, *refs):
    outs, (code_ref,) = cut(refs, count_of(SP_IN[0]))
    half = TOK // 2
    code_rows = []
    for source in range(PARTS):
        note = x_ref[source, TOK + half : TOK + half + 16, :].astype(jnp.float32)
        note = note[:1].astype(jnp.int32)
        code_rows.append(note[:, :TOK] * TOK + note[:, TOK : 2 * TOK])
        code_ref[source : source + 1, :] = code_rows[-1]
    pair_rows = jnp.concatenate(
        [
            x_ref[source, TOK : TOK + half, 2 * HEAD * part : 2 * HEAD * (part + 1)]
            for source in range(PARTS)
            for part in range(2)
        ],
        axis=0,
    )
    rows = x_ref[:, :TOK, :].reshape(QUARTER, x_ref.shape[2])
    rows = jnp.concatenate([rows, pair_rows], axis=1)
    for owner, block in view(outs, spot_ref[1], 1):
        block[...] = dot(hot_rows(code_rows, owner), rows, 1, 0).astype(jnp.bfloat16)


def place_first(spot, field, *after):
    width = field.shape[2] + 2 * HEAD
    outs = call(
        place_first_body,
        shapes_of(SP_IN[0], TOK, width) + [jax.ShapeDtypeStruct((PARTS, TOK), jnp.int32)],
        (spot, field, *after),
        [IN_SMEM, IN_VMEM, UNTOUCHED, UNTOUCHED],
        2 * QUARTER * QUARTER * width,
    )
    return unwrap(outs[:-1]), outs[-1]


def place_body(count, after, spot_ref, code_ref, *refs):
    refs, _, outs = cut(refs, count, after)
    blocks = view(refs, spot_ref[0], -1)
    rows = jnp.concatenate([block[...] for _, block in blocks], axis=0)
    code_rows = [code_ref[pl.ds(owner, 1), :] for owner, _ in blocks]
    for owner, block in view(outs, spot_ref[1], 1):
        hot = hot_rows(code_rows, owner)
        block[...] = dot(hot, rows, 1, 0).astype(jnp.bfloat16)


def place(spot, code, field, ring, after=()):
    field = flat(field)
    width = field[0].shape[-1]
    return unwrap(
        call(
            functools.partial(place_body, len(field), len(after)),
            shapes_of(ring, TOK, width),
            (spot, code, *field, *after),
            [IN_SMEM] + [IN_VMEM] * (1 + len(field)) + [UNTOUCHED] * len(after),
            2 * QUARTER * QUARTER * width,
        )
    )


def unplace_body(count, after, spot_ref, code_ref, *refs):
    main, _, outs = cut(refs, count, after)
    blocks = view(main, spot_ref[1], -1)
    lane = lax.broadcasted_iota(jnp.int32, (1, TOK), 1)
    spots = jnp.concatenate([lane + owner * TOK for owner, _ in blocks], axis=1)
    rows = jnp.concatenate([block[...] for _, block in blocks], axis=0)
    for owner, block in view(outs, spot_ref[0], 1):
        hot = jnp.where(code_ref[owner] == spots, 1.0, 0.0).astype(jnp.bfloat16)
        block[...] = dot(hot, rows, 1, 0).astype(jnp.bfloat16)


def unplace(spot, code_columns, ring, main, after=()):
    main = flat(main)
    width = main[0].shape[-1]
    return unwrap(
        call(
            functools.partial(unplace_body, len(main), len(after)),
            shapes_of(ring, TOK, width),
            (spot, code_columns, *main, *after),
            [IN_SMEM] + [IN_VMEM] * (1 + len(main)) + [UNTOUCHED] * len(after),
            2 * QUARTER * QUARTER * width,
        )
    )


def finish_body(counts, spot_ref, *refs):
    *homes, pairs, (out_ref, q_ref, k_ref, v_ref, pair_ref) = cut(refs, *counts)
    for chunk, home in enumerate(homes):
        for owner, block in view(home, spot_ref[0], -1):
            width = block.shape[1] // 2
            columns = columns_of(owner * CHUNKS + chunk, width)
            out_ref[:, columns] = block[:, :width]
            q_ref[:, columns] = block[:, width:]
    for owner, block in view(pairs, spot_ref[0], -1):
        pair_ref[owner] = block[...]
    for head in range(PARTS // 2):
        columns = pl.ds(head * HEAD, HEAD)
        pair = pair_ref[2 * head].astype(jnp.float32) + pair_ref[2 * head + 1].astype(jnp.float32)
        k_ref[:, columns] = pair[:, :HEAD].astype(jnp.bfloat16)
        v_ref[:, columns] = pair[:, HEAD:].astype(jnp.bfloat16)


def finish(spot, homes, wide, narrow):
    homes = [flat(home) for home in homes]
    args = [block for home in homes for block in home]
    return call(
        functools.partial(finish_body, [len(home) for home in homes]),
        [
            jax.ShapeDtypeStruct((TOK, width), jnp.bfloat16)
            for width in (wide, wide, narrow, narrow)
        ],
        (spot, *args),
        [IN_SMEM] + [IN_VMEM] * len(args),
        1 << 20,
        (pltpu.VMEM((PARTS, TOK, 2 * HEAD), jnp.bfloat16),),
    )


def settle_body(after, spot_ref, own_ref, spilled_ref, *refs):
    _, outs = cut(refs, after)
    for owner, block in view(outs, spot_ref[1], 1):
        at = rows_of(owner)
        block[...] = (own_ref[at, :] + spilled_ref[at, :].astype(jnp.float32)).astype(jnp.bfloat16)


def settle(spot, own, spilled, after):
    return unwrap(
        call(
            functools.partial(settle_body, len(after)),
            shapes_of(SP_OUT[-1], TOK, 2 * HEAD),
            (spot, own, spilled, *after),
            [IN_SMEM, IN_VMEM, IN_VMEM] + [UNTOUCHED] * len(after),
            1 << 20,
        )
    )


def wide_tables(table):
    left = lax.broadcasted_iota(jnp.int32, table.shape, 1) < HEAD // 2
    other = pltpu.roll(table, HEAD // 2, 1)
    return jnp.where(left, table, other), jnp.where(left, -other, table)


def turn(field, cosine, sine):
    return field * cosine + pltpu.roll(field, HEAD // 2, 1) * sine


def ready_body(spot_ref, own_ref, before_ref, table_ref, k_ref, v_ref):
    for half, source in ((0, before_ref), (1, own_ref)):
        for owner, block in view([source], spot_ref[1], -1, rotated=SP_IN[0]):
            at = rows_of(owner, half)
            cosine, sine = wide_tables(table_ref[at, :])
            k_ref[at, :] = turn(block[:, :HEAD].astype(jnp.float32), cosine, sine).astype(
                jnp.bfloat16
            )
            v_ref[at, :] = block[:, HEAD:]


def ready(spot, own, before, table):
    return call(
        ready_body,
        [jax.ShapeDtypeStruct((2 * QUARTER, HEAD), jnp.bfloat16)] * 2,
        (spot, own, before, table),
        [IN_SMEM] + [IN_VMEM] * 3,
        1 << 20,
    )


def attend_body(heads, last, count, after, ring, spot_ref, starts_ref, k_hbm, v_hbm, table_hbm, *refs):
    scale = 1.0 / math.sqrt(HEAD)
    rows = heads * BLOCK_Q
    blocks, old_refs, _, outs, sums, refs = cut(
        refs, count, 1 if last else 0, after, count_of(ring), 1
    )
    qg_ref, og_ref, dkv_ref, k_rot, v_all, table_ref, q_rot, g_all, q_turned, g_turned, s_ref, p_ref, d_ref, sem = refs
    team = spot_ref[1]
    pairs = [
        (block.at[:, pl.ds(0, qg_ref.shape[1])], qg_ref.at[rows_of(owner), :])
        for owner, block in view(blocks, team, -1)
    ]
    pairs += [(k_hbm, k_rot), (v_hbm, v_all)]
    pairs.append((table_hbm.at[pl.ds(QUARTER, QUARTER), :], table_ref))
    if last:
        pairs.append((old_refs[0], dkv_ref))
    copies = [
        pltpu.make_async_copy(source, target, sem.at[index])
        for index, (source, target) in enumerate(pairs)
    ]
    for copy in copies:
        copy.start()
    if not last:
        dkv_ref[...] = jnp.zeros_like(dkv_ref)
    for copy in copies:
        copy.wait()

    def attend_block(size, low, start, end, cosine, sine):
        here = pl.ds(low, BLOCK_Q)
        wide = size * BLOCK_K
        window = pl.ds(pl.multiple_of(low + (SPAN - size) * BLOCK_K, BLOCK_K), wide)
        key = lax.broadcasted_iota(jnp.int32, (BLOCK_Q, wide), 1) + (low + (SPAN - size) * BLOCK_K)
        allowed = (key >= start) & (key <= end)
        for head in range(heads):
            at = pl.ds(head * BLOCK_Q, BLOCK_Q)
            score = jnp.where(allowed, dot(q_rot[at, :], k_rot[window, :], 1, 1), -jnp.inf)
            top = jnp.max(score, axis=1, keepdims=True)
            weight = jnp.exp2((score - top) * (scale * LOG2E))
            weight = weight * (1.0 / jnp.sum(weight, axis=1, keepdims=True))
            weight_low = weight.astype(jnp.bfloat16)
            p_ref[at, :wide] = weight_low
            s_ref[at, :wide] = weight
            mixed = dot(weight_low, v_all[window, :], 1, 0)
            og_ref[here, pl.ds(head * HEAD, HEAD)] = mixed.astype(jnp.bfloat16)
            g_rows = g_all[at, :]
            delta = jnp.sum(g_rows.astype(jnp.float32) * mixed, axis=1, keepdims=True)
            weight_grad = dot(g_rows, v_all[window, :], 1, 1)
            score_grad = (s_ref[at, :wide] * (weight_grad - delta)).astype(jnp.bfloat16)
            d_ref[at, :wide] = score_grad
            q_grad = dot(score_grad, k_rot[window, :], 1, 0)
            dkv_ref[HEAD:, window] += dot(g_turned[:, at], p_ref[at, :wide], 1, 0)
            dkv_ref[:HEAD, window] += dot(q_turned[:, at], d_ref[at, :wide], 1, 0)
            og_ref[here, pl.ds((heads + head) * HEAD, HEAD)] = turn(
                q_grad * scale, cosine, -sine
            ).astype(jnp.bfloat16)

    @pl.loop(0, QUARTER // BLOCK_Q)
    def _(block):
        low = pl.multiple_of(block * BLOCK_Q, BLOCK_Q)
        here = pl.ds(low, BLOCK_Q)
        cosine, sine = wide_tables(table_ref[here, :])
        for head in range(heads):
            at = pl.ds(head * BLOCK_Q, BLOCK_Q)
            query = qg_ref[here, pl.ds(head * HEAD, HEAD)].astype(jnp.float32)
            q_rot[at, :] = turn(query, cosine, sine).astype(jnp.bfloat16)
            g_all[at, :] = qg_ref[here, pl.ds((heads + head) * HEAD, HEAD)]
        end = lax.broadcasted_iota(jnp.int32, (BLOCK_Q, 1), 0) + (QUARTER + low)
        start = jnp.zeros((BLOCK_Q, 1), jnp.int32)
        first = 0
        for index in range(starts_ref.shape[0]):
            begin = starts_ref[index]
            start = jnp.where(end >= begin, begin, start)
            first = jnp.where(QUARTER + low >= begin, begin, first)
        count = (QUARTER + low + BLOCK_Q - first + BLOCK_K - 1) // BLOCK_K
        q_turned[...] = jnp.transpose(q_rot[...])
        g_turned[...] = jnp.transpose(g_all[...])
        for size in range(1, SPAN + 1):
            pl.when(count == size)(functools.partial(attend_block, size, low, start, end, cosine, sine))

    pairs = [(og_ref.at[rows_of(owner), :], block) for owner, block in view(outs, team, 1)]
    pairs.append((dkv_ref, sums[0]))
    copies = [
        pltpu.make_async_copy(source, target, sem.at[index])
        for index, (source, target) in enumerate(pairs)
    ]
    for copy in copies:
        copy.start()
    for copy in copies:
        copy.wait()


def attend(heads, ring, spot, starts, keys, values, table, blocks, old, after=()):
    rows = heads * BLOCK_Q
    last = old is not None
    wide = 2 * heads * HEAD
    blocks = flat(blocks)
    sums = [jax.ShapeDtypeStruct((2 * HEAD, 2 * QUARTER), jnp.float32)]
    args = [spot, starts, keys, values, table, *blocks] + ([old] if last else [])
    shapes = shapes_of(ring, TOK, wide) + sums
    outs = pl.pallas_call(
        functools.partial(attend_body, heads, last, len(blocks), len(after), ring),
        out_shape=shapes,
        in_specs=[IN_SMEM, IN_SMEM] + [UNTOUCHED] * (len(args) - 2 + len(after)),
        out_specs=[UNTOUCHED] * len(shapes),
        scratch_shapes=(
            pltpu.VMEM((QUARTER, wide), jnp.bfloat16),
            pltpu.VMEM((QUARTER, wide), jnp.bfloat16),
            pltpu.VMEM((2 * HEAD, 2 * QUARTER), jnp.float32),
            pltpu.VMEM((2 * QUARTER, HEAD), jnp.bfloat16),
            pltpu.VMEM((2 * QUARTER, HEAD), jnp.bfloat16),
            pltpu.VMEM((QUARTER, HEAD), jnp.float32),
            pltpu.VMEM((rows, HEAD), jnp.bfloat16),
            pltpu.VMEM((rows, HEAD), jnp.bfloat16),
            pltpu.VMEM((HEAD, rows), jnp.bfloat16),
            pltpu.VMEM((HEAD, rows), jnp.bfloat16),
            pltpu.VMEM((rows, SPAN * BLOCK_K), jnp.float32),
            pltpu.VMEM((rows, SPAN * BLOCK_K), jnp.bfloat16),
            pltpu.VMEM((rows, SPAN * BLOCK_K), jnp.bfloat16),
            pltpu.SemaphoreType.DMA((PARTS + 6,)),
        ),
        compiler_params=pltpu.CompilerParams(vmem_limit_bytes=PACK_VMEM),
        cost_estimate=pl.CostEstimate(
            flops=ATTEND_FLOPS * heads, bytes_accessed=4 << 20, transcendentals=0
        ),
    )(*args, *after)
    blocks, sums = cut(outs, count_of(ring))
    return unwrap(blocks), sums[0]


def spill_body(sum_ref, table_ref, _, spill_ref, keep_ref):
    scale = 1.0 / math.sqrt(HEAD)
    sums = jnp.transpose(sum_ref[...])
    cosine, sine = wide_tables(table_ref[...])
    turned = turn(sums[:, :HEAD] * scale, cosine, -sine)
    spill_ref[:, :HEAD] = turned[:QUARTER].astype(jnp.bfloat16)
    spill_ref[:, HEAD:] = sums[:QUARTER, HEAD:].astype(jnp.bfloat16)
    keep_ref[:, :HEAD] = turned[QUARTER:]
    keep_ref[:, HEAD:] = sums[QUARTER:, HEAD:]


def spill(sums, table, after):
    return call(
        spill_body,
        [
            jax.ShapeDtypeStruct((QUARTER, 2 * HEAD), jnp.bfloat16),
            jax.ShapeDtypeStruct((QUARTER, 2 * HEAD), jnp.float32),
        ],
        (sums, table, after),
        [IN_VMEM, IN_VMEM, UNTOUCHED],
        1 << 20,
    )


def tie_body(count, *refs):
    pass


def tie(field, *after):
    parts = flat(field)
    outs = pl.pallas_call(
        functools.partial(tie_body, len(parts)),
        out_shape=[jax.ShapeDtypeStruct(part.shape, part.dtype) for part in parts],
        in_specs=[UNTOUCHED] * (len(parts) + len(after)),
        out_specs=[UNTOUCHED] * len(parts),
        input_output_aliases={index: index for index in range(len(parts))},
        cost_estimate=pl.CostEstimate(flops=1, bytes_accessed=1, transcendentals=0),
    )(*parts, *after)
    return unwrap(list(outs))


def exchange(field, axis):
    size = lax.axis_size(axis)
    if not isinstance(field, list):
        teams = [[low + index for index in range(PARTS)] for low in range(0, size, PARTS)]
        return lax.all_to_all(
            field, axis, split_axis=0, concat_axis=0, tiled=True, axis_index_groups=teams
        )
    got = {0: field[0]}
    for step in (4, 3, 5, 2, 6, 1, 7):
        pairs = [
            (index, index - index % PARTS + (index % PARTS + step) % PARTS) for index in range(size)
        ]
        got[step] = lax.ppermute(field[step], axis, pairs)
    return [got[step] for step in range(PARTS)]


def shift(field, step):
    size = lax.axis_size("sp")
    return lax.ppermute(field, "sp", [(index, (index + step) % size) for index in range(size)])


def tables(group_lengths):
    index = lax.axis_index("sp")
    lengths = lax.dynamic_index_in_dim(group_lengths, index % PARTS, 0, keepdims=False)
    starts = jnp.cumsum(lengths) - lengths - (index // PARTS - 1) * QUARTER
    rows = jnp.arange(2 * QUARTER, dtype=jnp.int32)[:, None]
    begin = jnp.max(jnp.where(rows >= starts[None, :], starts[None, :], -QUARTER), axis=1)
    position = rows[:, 0] - jnp.maximum(begin, -QUARTER)
    freq = jnp.power(500000.0, -(2.0 / HEAD) * jnp.arange(HEAD // 2, dtype=jnp.float32))
    angle = position.astype(jnp.float32)[:, None] * freq[None, :]
    return starts, jnp.concatenate([jnp.cos(angle), jnp.sin(angle)], axis=1)


def shards(queries, keys, values, out_grad, dest_group, dest_slot, group_lengths):
    heads = queries.shape[1] // HEAD // lax.axis_size("grp") // CHUNKS
    spot = jnp.stack([lax.axis_index("grp"), lax.axis_index("sp") % PARTS]).astype(jnp.int32)
    note = jnp.concatenate([dest_group, dest_slot]).astype(jnp.bfloat16)
    note = jnp.broadcast_to(jnp.concatenate([note, note])[None, :], (16, 4 * HEAD))
    first = exchange(pack(0, queries, out_grad, keys, values, note), "grp")
    second = exchange(pack(1, queries, out_grad), "grp")
    starts, table = tables(group_lengths)
    first, code = place_first(spot, first, table, starts)
    code_columns = code[:, :, None]
    first = exchange(first, "sp")
    own = jnp.stack([block[:, -2 * HEAD :] for block in first])
    before = shift(own, PARTS)
    k_rot, v_all = ready(spot, own, before, table)
    fixed = (spot, starts, k_rot, v_all, table)
    second = place(spot, code, second, SP_IN[1])
    blocks, sums = attend(heads, SP_OUT[0], *fixed, first, None, after=flat(second)[:1])
    second = exchange(second, "sp")
    early = exchange(tie(blocks, flat(second)[-1]), "sp")
    blocks, sums = attend(heads, SP_OUT[1], *fixed, second, sums)
    early = unplace(spot, code_columns, Z_OUT[0], early, after=flat(blocks)[:1])
    early_home = exchange(early, "grp")
    spilled, keep = spill(sums, table, flat(early)[0])
    spilled = shift(spilled, -PARTS)
    blocks = exchange(blocks, "sp")
    pairs = settle(spot, keep, spilled, flat(blocks))
    if PAIRS_FIRST:
        pairs = unplace(spot, code_columns, Z_OUT[2], exchange(pairs, "sp"))
    late = unplace(
        spot, code_columns, Z_OUT[1], blocks, after=flat(early_home)[:1] + flat(pairs)[:1]
    )
    if not PAIRS_FIRST:
        pairs = unplace(spot, code_columns, Z_OUT[2], exchange(pairs, "sp"))
    homes = [early_home, exchange(late, "grp"), exchange(pairs, "grp")]
    return tuple(finish(spot, homes, queries.shape[1], keys.shape[1]))


def solution(mesh):
    rows = P(("grp", "sp"), None)
    flat = P(("grp", "sp"))
    return jax.shard_map(
        shards,
        mesh=mesh,
        in_specs=(rows, rows, rows, rows, flat, flat, P()),
        out_specs=(rows, rows, rows, rows),
        check_vma=False,
    )
```

```python
import functools
import math

import jax
import jax.numpy as jnp
from jax import lax
from jax.experimental import pallas as pl
from jax.experimental.pallas import tpu as pltpu
from jax.sharding import PartitionSpec as P

HEAD = 128
TOK = 128
PARTS = 8
QUARTER = PARTS * TOK
BLOCK_Q = 256
BLOCK_K = 256
SPAN = QUARTER // BLOCK_K + 1
LOG2E = 1.0 / math.log(2.0)
CHUNKS = 2
SP_IN = (True, False)
SP_OUT = (False, True, True)
Z_OUT = (False, False, True)
PAIRS_FIRST = False
ATTEND_FLOPS = 8 * 10**9
VMEM = 48 * 1024 * 1024
PACK_VMEM = 60 * 1024 * 1024


def dot(left, right, left_dim, right_dim):
    return lax.dot_general(
        left, right, (((left_dim,), (right_dim,)), ((), ())), preferred_element_type=jnp.float32
    )


def call(body, out_shape, args, specs, flops, scratch=()):
    return pl.pallas_call(
        body,
        out_shape=out_shape,
        in_specs=specs,
        out_specs=jax.tree.map(lambda _: pl.BlockSpec(memory_space=pltpu.VMEM), out_shape),
        scratch_shapes=scratch,
        compiler_params=pltpu.CompilerParams(vmem_limit_bytes=VMEM),
        cost_estimate=pl.CostEstimate(flops=flops, bytes_accessed=4 << 20, transcendentals=0),
    )(*args)


IN_VMEM = pl.BlockSpec(memory_space=pltpu.VMEM)
IN_SMEM = pl.BlockSpec(memory_space=pltpu.SMEM)
UNTOUCHED = pl.BlockSpec(memory_space=pl.ANY)


def flat(field):
    return list(field) if isinstance(field, (list, tuple)) else [field]


def in_ring(base, step):
    return lax.rem(base + (step + PARTS), PARTS)


def view(refs, base, sign, rotated=None):
    if rotated is None:
        rotated = len(refs) > 1
    blocks = refs if len(refs) > 1 else [refs[0].at[step] for step in range(PARTS)]
    return [
        (in_ring(base, sign * step) if rotated else step, block)
        for step, block in enumerate(blocks)
    ]


def rows_of(owner, half=0):
    if isinstance(owner, int):
        return pl.ds(half * QUARTER + owner * TOK, TOK)
    return pl.ds(pl.multiple_of(half * QUARTER + owner * TOK, TOK), TOK)


def columns_of(owner, width, offset=0):
    if isinstance(owner, int):
        return pl.ds(owner * width + offset, width)
    return pl.ds(pl.multiple_of(owner * width + offset, HEAD), width)


def shapes_of(ring, rows, width, kind=jnp.bfloat16):
    if ring:
        return [jax.ShapeDtypeStruct((rows, width), kind)] * PARTS
    return [jax.ShapeDtypeStruct((PARTS, rows, width), kind)]


def cut(refs, *counts):
    parts = []
    for count in counts:
        parts.append(refs[:count])
        refs = refs[count:]
    return parts + [refs]


def count_of(ring):
    return PARTS if ring else 1


def unwrap(outs):
    return list(outs) if len(outs) > 1 else outs[0]


def pack_body(chunk, count, q_hbm, g_hbm, *refs):
    extra, (out, sem) = cut(refs, count)
    width = out.shape[2] // 2
    half = TOK // 2
    copies = []
    for plane in range(PARTS):
        columns = pl.ds((plane * CHUNKS + chunk) * width, width)
        copies.append((q_hbm.at[:, columns], out.at[plane, pl.ds(0, TOK), pl.ds(0, width)]))
        copies.append((g_hbm.at[:, columns], out.at[plane, pl.ds(0, TOK), pl.ds(width, width)]))
        if extra:
            k_hbm, v_hbm, note_hbm = extra
            columns = pl.ds(plane // 2 * HEAD, HEAD)
            for part in range(2):
                rows = pl.ds(part * half, half)
                for index, field in enumerate((k_hbm, v_hbm)):
                    there = pl.ds((2 * part + index) * HEAD, HEAD)
                    copies.append((field.at[rows, columns], out.at[plane, pl.ds(TOK, half), there]))
            copies.append((note_hbm, out.at[plane, pl.ds(TOK + half, 16), :]))
    copies = [
        pltpu.make_async_copy(source, target, sem.at[index])
        for index, (source, target) in enumerate(copies)
    ]
    for copy in copies:
        copy.start()
    for copy in copies:
        copy.wait()


def pack(chunk, queries, out_grad, *extra):
    width = 2 * queries.shape[1] // PARTS // CHUNKS
    depth = TOK + (TOK // 2 + 16 if extra else 0)
    return pl.pallas_call(
        functools.partial(pack_body, chunk, len(extra)),
        out_shape=jax.ShapeDtypeStruct((PARTS, depth, width), jnp.bfloat16),
        in_specs=[UNTOUCHED] * (2 + len(extra)),
        out_specs=IN_VMEM,
        scratch_shapes=[pltpu.SemaphoreType.DMA((PARTS * 7,))],
        compiler_params=pltpu.CompilerParams(vmem_limit_bytes=PACK_VMEM),
        cost_estimate=pl.CostEstimate(flops=1 << 20, bytes_accessed=4 << 20, transcendentals=0),
    )(queries, out_grad, *extra)


def hot_rows(code_rows, group):
    slots = lax.broadcasted_iota(jnp.int32, (TOK, TOK), 0) + group * TOK
    return jnp.concatenate(
        [jnp.where(slots == row, 1.0, 0.0) for row in code_rows], axis=1
    ).astype(jnp.bfloat16)


def place_first_body(spot_ref, x_ref, _, __, *refs):
    outs, (code_ref,) = cut(refs, count_of(SP_IN[0]))
    half = TOK // 2
    code_rows = []
    for source in range(PARTS):
        note = x_ref[source, TOK + half : TOK + half + 16, :].astype(jnp.float32)
        note = note[:1].astype(jnp.int32)
        code_rows.append(note[:, :TOK] * TOK + note[:, TOK : 2 * TOK])
        code_ref[source : source + 1, :] = code_rows[-1]
    pair_rows = jnp.concatenate(
        [
            x_ref[source, TOK : TOK + half, 2 * HEAD * part : 2 * HEAD * (part + 1)]
            for source in range(PARTS)
            for part in range(2)
        ],
        axis=0,
    )
    rows = x_ref[:, :TOK, :].reshape(QUARTER, x_ref.shape[2])
    rows = jnp.concatenate([rows, pair_rows], axis=1)
    for owner, block in view(outs, spot_ref[1], 1):
        block[...] = dot(hot_rows(code_rows, owner), rows, 1, 0).astype(jnp.bfloat16)


def place_first(spot, field, *after):
    width = field.shape[2] + 2 * HEAD
    outs = call(
        place_first_body,
        shapes_of(SP_IN[0], TOK, width) + [jax.ShapeDtypeStruct((PARTS, TOK), jnp.int32)],
        (spot, field, *after),
        [IN_SMEM, IN_VMEM, UNTOUCHED, UNTOUCHED],
        2 * QUARTER * QUARTER * width,
    )
    return unwrap(outs[:-1]), outs[-1]


def place_body(count, after, spot_ref, code_ref, *refs):
    refs, _, outs = cut(refs, count, after)
    blocks = view(refs, spot_ref[0], -1)
    rows = jnp.concatenate([block[...] for _, block in blocks], axis=0)
    code_rows = [code_ref[pl.ds(owner, 1), :] for owner, _ in blocks]
    for owner, block in view(outs, spot_ref[1], 1):
        hot = hot_rows(code_rows, owner)
        block[...] = dot(hot, rows, 1, 0).astype(jnp.bfloat16)


def place(spot, code, field, ring, after=()):
    field = flat(field)
    width = field[0].shape[-1]
    return unwrap(
        call(
            functools.partial(place_body, len(field), len(after)),
            shapes_of(ring, TOK, width),
            (spot, code, *field, *after),
            [IN_SMEM] + [IN_VMEM] * (1 + len(field)) + [UNTOUCHED] * len(after),
            2 * QUARTER * QUARTER * width,
        )
    )


def unplace_body(count, after, spot_ref, code_ref, *refs):
    main, _, outs = cut(refs, count, after)
    blocks = view(main, spot_ref[1], -1)
    lane = lax.broadcasted_iota(jnp.int32, (1, TOK), 1)
    spots = jnp.concatenate([lane + owner * TOK for owner, _ in blocks], axis=1)
    rows = jnp.concatenate([block[...] for _, block in blocks], axis=0)
    for owner, block in view(outs, spot_ref[0], 1):
        hot = jnp.where(code_ref[owner] == spots, 1.0, 0.0).astype(jnp.bfloat16)
        block[...] = dot(hot, rows, 1, 0).astype(jnp.bfloat16)


def unplace(spot, code_columns, ring, main, after=()):
    main = flat(main)
    width = main[0].shape[-1]
    return unwrap(
        call(
            functools.partial(unplace_body, len(main), len(after)),
            shapes_of(ring, TOK, width),
            (spot, code_columns, *main, *after),
            [IN_SMEM] + [IN_VMEM] * (1 + len(main)) + [UNTOUCHED] * len(after),
            2 * QUARTER * QUARTER * width,
        )
    )


def finish_body(counts, spot_ref, *refs):
    *homes, pairs, (out_ref, q_ref, k_ref, v_ref, pair_ref) = cut(refs, *counts)
    for chunk, home in enumerate(homes):
        for owner, block in view(home, spot_ref[0], -1):
            width = block.shape[1] // 2
            columns = columns_of(owner * CHUNKS + chunk, width)
            out_ref[:, columns] = block[:, :width]
            q_ref[:, columns] = block[:, width:]
    for owner, block in view(pairs, spot_ref[0], -1):
        pair_ref[owner] = block[...]
    for head in range(PARTS // 2):
        columns = pl.ds(head * HEAD, HEAD)
        pair = pair_ref[2 * head].astype(jnp.float32) + pair_ref[2 * head + 1].astype(jnp.float32)
        k_ref[:, columns] = pair[:, :HEAD].astype(jnp.bfloat16)
        v_ref[:, columns] = pair[:, HEAD:].astype(jnp.bfloat16)


def finish(spot, homes, wide, narrow):
    homes = [flat(home) for home in homes]
    args = [block for home in homes for block in home]
    return call(
        functools.partial(finish_body, [len(home) for home in homes]),
        [
            jax.ShapeDtypeStruct((TOK, width), jnp.bfloat16)
            for width in (wide, wide, narrow, narrow)
        ],
        (spot, *args),
        [IN_SMEM] + [IN_VMEM] * len(args),
        1 << 20,
        (pltpu.VMEM((PARTS, TOK, 2 * HEAD), jnp.bfloat16),),
    )


def settle_body(after, spot_ref, own_ref, spilled_ref, *refs):
    _, outs = cut(refs, after)
    for owner, block in view(outs, spot_ref[1], 1):
        at = rows_of(owner)
        block[...] = (own_ref[at, :] + spilled_ref[at, :].astype(jnp.float32)).astype(jnp.bfloat16)


def settle(spot, own, spilled, after):
    return unwrap(
        call(
            functools.partial(settle_body, len(after)),
            shapes_of(SP_OUT[-1], TOK, 2 * HEAD),
            (spot, own, spilled, *after),
            [IN_SMEM, IN_VMEM, IN_VMEM] + [UNTOUCHED] * len(after),
            1 << 20,
        )
    )


def wide_tables(table):
    left = lax.broadcasted_iota(jnp.int32, table.shape, 1) < HEAD // 2
    other = pltpu.roll(table, HEAD // 2, 1)
    return jnp.where(left, table, other), jnp.where(left, -other, table)


def turn(field, cosine, sine):
    return field * cosine + pltpu.roll(field, HEAD // 2, 1) * sine


def ready_body(spot_ref, own_ref, before_ref, table_ref, k_ref, v_ref):
    for half, source in ((0, before_ref), (1, own_ref)):
        for owner, block in view([source], spot_ref[1], -1, rotated=SP_IN[0]):
            at = rows_of(owner, half)
            cosine, sine = wide_tables(table_ref[at, :])
            k_ref[at, :] = turn(block[:, :HEAD].astype(jnp.float32), cosine, sine).astype(
                jnp.bfloat16
            )
            v_ref[at, :] = block[:, HEAD:]


def ready(spot, own, before, table):
    return call(
        ready_body,
        [jax.ShapeDtypeStruct((2 * QUARTER, HEAD), jnp.bfloat16)] * 2,
        (spot, own, before, table),
        [IN_SMEM] + [IN_VMEM] * 3,
        1 << 20,
    )


def attend_body(heads, last, count, after, ring, spot_ref, starts_ref, k_hbm, v_hbm, table_hbm, *refs):
    scale = 1.0 / math.sqrt(HEAD)
    rows = heads * BLOCK_Q
    blocks, old_refs, _, outs, sums, refs = cut(
        refs, count, 1 if last else 0, after, count_of(ring), 1
    )
    qg_ref, og_ref, dkv_ref, k_rot, v_all, table_ref, q_rot, g_all, q_turned, g_turned, s_ref, p_ref, d_ref, sem = refs
    team = spot_ref[1]
    pairs = [
        (block.at[:, pl.ds(0, qg_ref.shape[1])], qg_ref.at[rows_of(owner), :])
        for owner, block in view(blocks, team, -1)
    ]
    pairs += [(k_hbm, k_rot), (v_hbm, v_all)]
    pairs.append((table_hbm.at[pl.ds(QUARTER, QUARTER), :], table_ref))
    if last:
        pairs.append((old_refs[0], dkv_ref))
    copies = [
        pltpu.make_async_copy(source, target, sem.at[index])
        for index, (source, target) in enumerate(pairs)
    ]
    for copy in copies:
        copy.start()
    if not last:
        dkv_ref[...] = jnp.zeros_like(dkv_ref)
    for copy in copies:
        copy.wait()

    def attend_block(size, low, start, end, cosine, sine):
        here = pl.ds(low, BLOCK_Q)
        wide = size * BLOCK_K
        window = pl.ds(pl.multiple_of(low + (SPAN - size) * BLOCK_K, BLOCK_K), wide)
        key = lax.broadcasted_iota(jnp.int32, (BLOCK_Q, wide), 1) + (low + (SPAN - size) * BLOCK_K)
        allowed = (key >= start) & (key <= end)
        for head in range(heads):
            at = pl.ds(head * BLOCK_Q, BLOCK_Q)
            score = jnp.where(allowed, dot(q_rot[at, :], k_rot[window, :], 1, 1), -jnp.inf)
            top = jnp.max(score, axis=1, keepdims=True)
            weight = jnp.exp2((score - top) * (scale * LOG2E))
            weight = weight * (1.0 / jnp.sum(weight, axis=1, keepdims=True))
            weight_low = weight.astype(jnp.bfloat16)
            p_ref[at, :wide] = weight_low
            s_ref[at, :wide] = weight
            mixed = dot(weight_low, v_all[window, :], 1, 0)
            og_ref[here, pl.ds(head * HEAD, HEAD)] = mixed.astype(jnp.bfloat16)
            g_rows = g_all[at, :]
            delta = jnp.sum(g_rows.astype(jnp.float32) * mixed, axis=1, keepdims=True)
            weight_grad = dot(g_rows, v_all[window, :], 1, 1)
            score_grad = (s_ref[at, :wide] * (weight_grad - delta)).astype(jnp.bfloat16)
            d_ref[at, :wide] = score_grad
            q_grad = dot(score_grad, k_rot[window, :], 1, 0)
            dkv_ref[HEAD:, window] += dot(g_turned[:, at], p_ref[at, :wide], 1, 0)
            dkv_ref[:HEAD, window] += dot(q_turned[:, at], d_ref[at, :wide], 1, 0)
            og_ref[here, pl.ds((heads + head) * HEAD, HEAD)] = turn(
                q_grad * scale, cosine, -sine
            ).astype(jnp.bfloat16)

    @pl.loop(0, QUARTER // BLOCK_Q)
    def _(block):
        low = pl.multiple_of(block * BLOCK_Q, BLOCK_Q)
        here = pl.ds(low, BLOCK_Q)
        cosine, sine = wide_tables(table_ref[here, :])
        for head in range(heads):
            at = pl.ds(head * BLOCK_Q, BLOCK_Q)
            query = qg_ref[here, pl.ds(head * HEAD, HEAD)].astype(jnp.float32)
            q_rot[at, :] = turn(query, cosine, sine).astype(jnp.bfloat16)
            g_all[at, :] = qg_ref[here, pl.ds((heads + head) * HEAD, HEAD)]
        end = lax.broadcasted_iota(jnp.int32, (BLOCK_Q, 1), 0) + (QUARTER + low)
        start = jnp.zeros((BLOCK_Q, 1), jnp.int32)
        first = 0
        for index in range(starts_ref.shape[0]):
            begin = starts_ref[index]
            start = jnp.where(end >= begin, begin, start)
            first = jnp.where(QUARTER + low >= begin, begin, first)
        count = (QUARTER + low + BLOCK_Q - first + BLOCK_K - 1) // BLOCK_K
        q_turned[...] = jnp.transpose(q_rot[...])
        g_turned[...] = jnp.transpose(g_all[...])
        for size in range(1, SPAN + 1):
            pl.when(count == size)(functools.partial(attend_block, size, low, start, end, cosine, sine))

    pairs = [(og_ref.at[rows_of(owner), :], block) for owner, block in view(outs, team, 1)]
    pairs.append((dkv_ref, sums[0]))
    copies = [
        pltpu.make_async_copy(source, target, sem.at[index])
        for index, (source, target) in enumerate(pairs)
    ]
    for copy in copies:
        copy.start()
    for copy in copies:
        copy.wait()


def attend(heads, ring, spot, starts, keys, values, table, blocks, old, after=()):
    rows = heads * BLOCK_Q
    last = old is not None
    wide = 2 * heads * HEAD
    blocks = flat(blocks)
    sums = [jax.ShapeDtypeStruct((2 * HEAD, 2 * QUARTER), jnp.float32)]
    args = [spot, starts, keys, values, table, *blocks] + ([old] if last else [])
    shapes = shapes_of(ring, TOK, wide) + sums
    outs = pl.pallas_call(
        functools.partial(attend_body, heads, last, len(blocks), len(after), ring),
        out_shape=shapes,
        in_specs=[IN_SMEM, IN_SMEM] + [UNTOUCHED] * (len(args) - 2 + len(after)),
        out_specs=[UNTOUCHED] * len(shapes),
        scratch_shapes=(
            pltpu.VMEM((QUARTER, wide), jnp.bfloat16),
            pltpu.VMEM((QUARTER, wide), jnp.bfloat16),
            pltpu.VMEM((2 * HEAD, 2 * QUARTER), jnp.float32),
            pltpu.VMEM((2 * QUARTER, HEAD), jnp.bfloat16),
            pltpu.VMEM((2 * QUARTER, HEAD), jnp.bfloat16),
            pltpu.VMEM((QUARTER, HEAD), jnp.float32),
            pltpu.VMEM((rows, HEAD), jnp.bfloat16),
            pltpu.VMEM((rows, HEAD), jnp.bfloat16),
            pltpu.VMEM((HEAD, rows), jnp.bfloat16),
            pltpu.VMEM((HEAD, rows), jnp.bfloat16),
            pltpu.VMEM((rows, SPAN * BLOCK_K), jnp.float32),
            pltpu.VMEM((rows, SPAN * BLOCK_K), jnp.bfloat16),
            pltpu.VMEM((rows, SPAN * BLOCK_K), jnp.bfloat16),
            pltpu.SemaphoreType.DMA((PARTS + 6,)),
        ),
        compiler_params=pltpu.CompilerParams(vmem_limit_bytes=PACK_VMEM),
        cost_estimate=pl.CostEstimate(
            flops=ATTEND_FLOPS * heads, bytes_accessed=4 << 20, transcendentals=0
        ),
    )(*args, *after)
    blocks, sums = cut(outs, count_of(ring))
    return unwrap(blocks), sums[0]


def spill_body(sum_ref, table_ref, _, spill_ref, keep_ref):
    scale = 1.0 / math.sqrt(HEAD)
    sums = jnp.transpose(sum_ref[...])
    cosine, sine = wide_tables(table_ref[...])
    turned = turn(sums[:, :HEAD] * scale, cosine, -sine)
    spill_ref[:, :HEAD] = turned[:QUARTER].astype(jnp.bfloat16)
    spill_ref[:, HEAD:] = sums[:QUARTER, HEAD:].astype(jnp.bfloat16)
    keep_ref[:, :HEAD] = turned[QUARTER:]
    keep_ref[:, HEAD:] = sums[QUARTER:, HEAD:]


def spill(sums, table, after):
    return call(
        spill_body,
        [
            jax.ShapeDtypeStruct((QUARTER, 2 * HEAD), jnp.bfloat16),
            jax.ShapeDtypeStruct((QUARTER, 2 * HEAD), jnp.float32),
        ],
        (sums, table, after),
        [IN_VMEM, IN_VMEM, UNTOUCHED],
        1 << 20,
    )


def tie_body(count, *refs):
    pass


def tie(field, *after):
    parts = flat(field)
    outs = pl.pallas_call(
        functools.partial(tie_body, len(parts)),
        out_shape=[jax.ShapeDtypeStruct(part.shape, part.dtype) for part in parts],
        in_specs=[UNTOUCHED] * (len(parts) + len(after)),
        out_specs=[UNTOUCHED] * len(parts),
        input_output_aliases={index: index for index in range(len(parts))},
        cost_estimate=pl.CostEstimate(flops=1, bytes_accessed=1, transcendentals=0),
    )(*parts, *after)
    return unwrap(list(outs))


def exchange(field, axis):
    size = lax.axis_size(axis)
    if not isinstance(field, list):
        teams = [[low + index for index in range(PARTS)] for low in range(0, size, PARTS)]
        return lax.all_to_all(
            field, axis, split_axis=0, concat_axis=0, tiled=True, axis_index_groups=teams
        )
    got = {0: field[0]}
    for step in (4, 3, 5, 2, 6, 1, 7):
        pairs = [
            (index, index - index % PARTS + (index % PARTS + step) % PARTS) for index in range(size)
        ]
        got[step] = lax.ppermute(field[step], axis, pairs)
    return [got[step] for step in range(PARTS)]


def shift(field, step):
    size = lax.axis_size("sp")
    return lax.ppermute(field, "sp", [(index, (index + step) % size) for index in range(size)])


def tables(group_lengths):
    index = lax.axis_index("sp")
    lengths = lax.dynamic_index_in_dim(group_lengths, index % PARTS, 0, keepdims=False)
    starts = jnp.cumsum(lengths) - lengths - (index // PARTS - 1) * QUARTER
    rows = jnp.arange(2 * QUARTER, dtype=jnp.int32)[:, None]
    begin = jnp.max(jnp.where(rows >= starts[None, :], starts[None, :], -QUARTER), axis=1)
    position = rows[:, 0] - jnp.maximum(begin, -QUARTER)
    freq = jnp.power(500000.0, -(2.0 / HEAD) * jnp.arange(HEAD // 2, dtype=jnp.float32))
    angle = position.astype(jnp.float32)[:, None] * freq[None, :]
    return starts, jnp.concatenate([jnp.cos(angle), jnp.sin(angle)], axis=1)


def shards(queries, keys, values, out_grad, dest_group, dest_slot, group_lengths):
    heads = queries.shape[1] // HEAD // lax.axis_size("grp") // CHUNKS
    spot = jnp.stack([lax.axis_index("grp"), lax.axis_index("sp") % PARTS]).astype(jnp.int32)
    note = jnp.concatenate([dest_group, dest_slot]).astype(jnp.bfloat16)
    note = jnp.broadcast_to(jnp.concatenate([note, note])[None, :], (16, 4 * HEAD))
    first = exchange(pack(0, queries, out_grad, keys, values, note), "grp")
    second = exchange(pack(1, queries, out_grad), "grp")
    starts, table = tables(group_lengths)
    first, code = place_first(spot, first, table, starts)
    code_columns = code[:, :, None]
    first = exchange(first, "sp")
    own = jnp.stack([block[:, -2 * HEAD :] for block in first])
    before = shift(own, PARTS)
    k_rot, v_all = ready(spot, own, before, table)
    fixed = (spot, starts, k_rot, v_all, table)
    second = place(spot, code, second, SP_IN[1])
    blocks, sums = attend(heads, SP_OUT[0], *fixed, first, None, after=flat(second)[:1])
    second = exchange(second, "sp")
    early = exchange(tie(blocks, flat(second)[-1]), "sp")
    blocks, sums = attend(heads, SP_OUT[1], *fixed, second, sums)
    early = unplace(spot, code_columns, Z_OUT[0], early, after=flat(blocks)[:1])
    early_home = exchange(early, "grp")
    spilled, keep = spill(sums, table, flat(early)[0])
    spilled = shift(spilled, -PARTS)
    blocks = exchange(blocks, "sp")
    pairs = settle(spot, keep, spilled, flat(blocks))
    if PAIRS_FIRST:
        pairs = unplace(spot, code_columns, Z_OUT[2], exchange(pairs, "sp"))
    late = unplace(
        spot, code_columns, Z_OUT[1], blocks, after=flat(early)[:1] + flat(pairs)[:1]
    )
    if not PAIRS_FIRST:
        pairs = unplace(spot, code_columns, Z_OUT[2], exchange(pairs, "sp"))
    homes = [early_home, exchange(late, "grp"), exchange(pairs, "grp")]
    return tuple(finish(spot, homes, queries.shape[1], keys.shape[1]))


def solution(mesh):
    rows = P(("grp", "sp"), None)
    flat = P(("grp", "sp"))
    return jax.shard_map(
        shards,
        mesh=mesh,
        in_specs=(rows, rows, rows, rows, flat, flat, P()),
        out_specs=(rows, rows, rows, rows),
        check_vma=False,
    )
```
